32 devices in a mesh: groups: 2 (over x), dom: 16 (over z, y, core).
Axes of the slice: x: 2, y: 2, z: 4, core: 2. Of those that a mesh axis runs over, the one named last changes fastest.
Arguments:
- blocks: float32 [1280, 4, 128, 128], P(('groups', 'dom')), parts along dimension 0, may hold values from -0.25 to 0.25
- offsets: int32 [1280, 4], P(('groups', 'dom')), parts along dimension 0, may hold values from -2 to 2, as said below
- diag_shift: float32 [163840], P(('groups', 'dom')), parts along dimension 0, may hold values from 1.2 to 2
- right_side: float32 [4, 163840], P(None, ('groups', 'dom')), parts along dimension 1, may hold values from -6 to 6
Outputs:
- solution: float32 [4, 163840], P(None, ('groups', 'dom')), parts along dimension 1
- residual: float32 [4, 163840], P(None, ('groups', 'dom')), parts along dimension 1
The draws below stay inside these ranges and needn't reach their ends.
There are 2 independent parts, one for each index of `groups`. The reference program is written for one: setup_inputs(seed, part) draws one part's arguments, and reference() takes and returns one part's arrays. A program takes and returns all parts, laid end to end along the dimension named above; each array names one. Nothing has to cross between parts.
Inputs may be any that keep to these rules, and one draw needn't show every extreme that they name: The first entry of each block row is 0, the diagonal block; the other 3 entries of a row are distinct nonzero offsets between -2 and 2.
All inputs are finite; a program needn't handle non-finite values.
Results may differ from the reference program's by a relative error of at most 0.0003.
Values sent between devices are 32-bit elements; how exact they have to be, the bound alone decides.
No kernel may reach another device: no remote copies, remote signals or barrier semaphores. Data moves between devices by JAX's collectives and lax.ppermute only.
A program may use at most 128 MiB of HBM per device.

```python
import math
import jax
import jax.numpy as jnp
from jax import lax

BS = 128
K = 4
W = 2
S = 6
NRHS = 4
CYCLES = 2
NB = 640
N = 81920


def draw_offsets(key, part):
    key = jax.random.fold_in(key, 11)
    row_keys = jax.random.split(key, NB)
    orders = jax.vmap(lambda one_key: jax.random.permutation(one_key, 2 * W))(row_keys)
    candidates = jnp.concatenate([jnp.arange(-W, 0), jnp.arange(1, W + 1)]).astype(jnp.int32)
    picked = candidates[orders[:, :K - 1]]
    return jnp.concatenate([jnp.zeros((NB, 1), jnp.int32), picked], axis=1).astype(jnp.int32)


def steps_of(rng, shape, cuts, low, top_value):
    gain, own = 1.0, jax.random.fold_in(rng, 6)
    for dim, blocks in cuts:
        heights = jnp.exp(jax.random.uniform(jax.random.fold_in(own, dim), (blocks,), jnp.float32, low / len(cuts), top_value / len(cuts)))
        gain = gain * jnp.repeat(heights, shape[dim] // blocks).reshape([-1 if axis == dim else 1 for axis in range(len(shape))])
    return gain


def noise(key, dims, spread, limit, shards=(), kind=jnp.bfloat16):
    drawn = spread * jax.random.normal(key, dims, jnp.float32)
    if shards:
        drawn = drawn * steps_of(key, dims, shards, -0.22, 0.18)
    return jnp.clip(drawn, -limit, limit).astype(kind)


def setup_inputs(seed: int = 0, part: int = 0) -> dict:
    key_list = jax.random.split(jax.random.key(seed), 5)
    own_keys = jax.random.split(jax.random.fold_in(key_list[4], part), 5)
    blocks = noise(own_keys[0], (NB, K, BS, BS), (K * BS) ** -0.5, 0.25, ((0, 16),), jnp.float32)
    offsets = draw_offsets(jax.random.fold_in(jax.random.fold_in(key_list[4], part), 71), part)
    diag_shift = jnp.clip(1.2 + 0.79999995 * jax.random.uniform(own_keys[2], (N,), jnp.float32) ** steps_of(own_keys[2], (N,), ((0, 16),), -0.2, 0.2), 1.2, 2.0)
    right_side = noise(own_keys[3], (NRHS, N), 1.0, 6.0, ((1, 16),), jnp.float32)
    return dict(blocks=blocks, offsets=offsets, diag_shift=diag_shift, right_side=right_side)


center_value = 1.6
half_range = 0.8

def newton_shifts():
    places = jnp.arange(S, dtype=jnp.float32)
    return center_value + half_range * jnp.cos(math.pi * (2.0 * places + 1.0) / (2.0 * S))

def with_diagonal(blocks, diag_shift):
    block_count = blocks.shape[0]
    block_size = blocks.shape[2]
    ident_block = jnp.eye(block_size, dtype=jnp.float32)
    diag_blocks = diag_shift.reshape(block_count, block_size)
    first = blocks[:, 0] + diag_blocks[:, :, None] * ident_block[None]
    return jnp.concatenate([first[:, None], blocks[:, 1:]], axis=1)

def apply_rows(matrix, pattern, region, count_rows, shift_value):
    column_index = jnp.arange(count_rows, dtype=jnp.int32)[:, None] + W + pattern
    gathered = region[:, column_index, :]
    product = jnp.einsum('ikab,rikb->ria', matrix, gathered, precision=lax.Precision.HIGHEST)
    return product - shift_value * region[:, W:W + count_rows, :]

def basis_matrix(shift_values):
    steps_count = shift_values.shape[0]
    places = jnp.arange(steps_count)
    bmat = jnp.zeros((steps_count + 1, steps_count), jnp.float32)
    bmat = bmat.at[places, places].set(shift_values)
    return bmat.at[places + 1, places].set(1.0)

def small_solve(gram, bmat):
    normal = jnp.einsum('ia,rij,jb->rab', bmat, gram, bmat, precision=lax.Precision.HIGHEST)
    target = jnp.einsum('ia,ri->ra', bmat, gram[:, :, 0], precision=lax.Precision.HIGHEST)
    lower = jnp.linalg.cholesky(normal)
    middle = lax.linalg.triangular_solve(lower, target[:, :, None], left_side=True, lower=True)
    coeffs = lax.linalg.triangular_solve(lower, middle, left_side=True, lower=True, transpose_a=True)[:, :, 0]
    unit = jnp.zeros((bmat.shape[0],), jnp.float32).at[0].set(1.0)
    combine = unit[None, :] - jnp.einsum('ja,ra->rj', bmat, coeffs, precision=lax.Precision.HIGHEST)
    return (coeffs, combine)

def reference(blocks, offsets, diag_shift, right_side):
    effective = with_diagonal(blocks, diag_shift)
    shift_values = newton_shifts()
    bmat = basis_matrix(shift_values)
    rhs_count = right_side.shape[0]
    solution = jnp.zeros_like(right_side)
    residual = right_side
    for cycle in range(CYCLES):
        vectors = [residual.reshape(rhs_count, NB, BS)]
        for step in range(S):
            padded = jnp.pad(vectors[-1], ((0, 0), (W, W), (0, 0)))
            vectors.append(apply_rows(effective, offsets, padded, NB, shift_values[step]))
        basis = jnp.stack(vectors, 1).reshape(rhs_count, S + 1, N)
        gram = jnp.einsum('rin,rjn->rij', basis, basis, precision=lax.Precision.HIGHEST)
        coeffs, combine = small_solve(gram, bmat)
        solution = solution + jnp.einsum('rj,rjn->rn', coeffs, basis[:, :S], precision=lax.Precision.HIGHEST)
        residual = jnp.einsum('rj,rjn->rn', combine, basis, precision=lax.Precision.HIGHEST)
    return (solution, residual)
```

```python
import functools
import math

import jax
import jax.numpy as jnp
import numpy as np
from jax import lax
from jax.experimental import pallas as pl
from jax.experimental.pallas import tpu as pltpu
from jax.sharding import PartitionSpec as P

W = 2
S = 6
CYCLES = 2
CHAIN = S * CYCLES
GROUPS = (2, 2, 2, 2, 2, 2)
SCALE = 0.125
GROW = 1.0 / SCALE
SHIFTS = [
    float(np.float32(1.6) + np.float32(0.8) * np.float32(math.cos(math.pi * (2 * j + 1) / (2 * S))))
    for j in range(S)
]
F32 = jnp.float32
BF16 = jnp.bfloat16
VM = pl.BlockSpec(memory_space=pltpu.VMEM)
SM = pl.BlockSpec(memory_space=pltpu.SMEM)
HB = pl.BlockSpec(memory_space=pltpu.HBM)


def params(mib):
    return pltpu.CompilerParams(vmem_limit_bytes=mib << 20)


def halves():
    return lax.broadcasted_iota(jnp.int32, (8, 128), 0) < 4


def split(tile, mask):
    high = tile.astype(BF16).astype(F32)
    return jnp.where(mask, high, tile - high)


def store_pair(block, high_ref, low_ref, pair, half, k):
    turned = block.T * SCALE
    high = turned.astype(BF16)
    low = (turned - high.astype(F32)).astype(BF16)
    rows, cols = slice(k * 128, (k + 1) * 128), slice(half * 128, (half + 1) * 128)
    high_ref[pair, rows, cols] = high
    low_ref[pair, rows, cols] = low


def prep_kernel(depth, margin, info, blocks, rhs, diag, offs, start, even, odd, sems):
    rows = diag.shape[0]
    parity = info[0]
    copies = []
    for place, (ref, at) in enumerate(((even, 1 - parity), (odd, parity))):
        first = pl.multiple_of(at * (rows - margin) * 512, 512)
        copies.append(
            pltpu.make_async_copy(
                blocks.at[pl.ds(first, margin * 512)],
                ref.at[pl.ds(0, margin * 512)],
                sems.at[place],
            )
        )
        copies[-1].start()
    for i in range(rows):
        part = rhs[:, i * 128 : (i + 1) * 128]
        start[i] = jnp.concatenate([part, part], 0)
    fill = jnp.zeros((margin, 124), F32)
    for ref, at in ((even, 1 - parity), (odd, parity)):
        base = margin * 512
        for i in range(depth):
            ref[base + 8 * i : base + 8 * i + 8, :] = start[at * (rows - depth) + i]
        base += 8 * depth
        is_high = at == 1
        diag_part = jnp.where(is_high, diag[rows - margin :, :], diag[:margin, :])
        offs_part = jnp.where(is_high, offs[rows - margin :, :], offs[:margin, :]).astype(F32)
        ref[base : base + margin, :] = diag_part
        ref[base + margin : base + 2 * margin, :] = jnp.concatenate([offs_part, fill], 1)
        if margin % 4:
            ref[base + 2 * margin : base + 8, :] = jnp.zeros((8 - 2 * margin, 128), F32)
    for copy in copies:
        copy.wait()


def convert_kernel(slots, blocks, high, low, buf, sems):
    rows = blocks.shape[0] // 512

    def fetch(i, slot):
        first = pl.multiple_of(i * 512, 512)
        return pltpu.make_async_copy(blocks.at[pl.ds(first, 512)], buf.at[slot], sems.at[slot])

    for slot in range(slots):
        fetch(slot, slot).start()

    def body(q, carry):
        for slot in range(slots):
            i = q * slots + slot
            fetch(i, slot).wait()
            for k in range(4):
                store_pair(
                    buf[slot, k * 128 : (k + 1) * 128, :],
                    high,
                    low,
                    q * (slots // 2) + slot // 2,
                    slot % 2,
                    k,
                )

            @pl.when(i + slots < rows)
            def _():
                fetch(i + slots, slot).start()

        return carry

    lax.fori_loop(0, rows // slots, body, 0)


def halo_kernel(depth, margin, info, even, odd, diag, high, low, scaled, halo):
    rows = diag.shape[0]
    parity = info[0]
    for i in range(rows):
        scaled[margin + i] = diag[i : i + 1, :] * SCALE
    for ref, side in ((even, 1 - parity), (odd, parity)):
        for m in range(margin):
            for k in range(4):
                first = (m * 4 + k) * 128
                store_pair(
                    ref[first : first + 128, :], high, low, side * (margin // 2) + m // 2, m % 2, k
                )
        base = margin * 512
        for i in range(depth):
            halo[side, i] = ref[base + 8 * i : base + 8 * i + 8, :]
        base += 8 * depth
        for m in range(margin):
            scaled[side * (rows + margin) + m] = ref[base + m : base + m + 1, :] * SCALE


def steps_kernel(first, steps, shifts, margin, next_depth, *refs):
    refs = list(refs)
    info, offs, high, low, halo_high, halo_low, scaled, own = refs[:8]
    del refs[:8]
    depth = W * steps
    if first:
        halo = refs.pop(0)
    else:
        from_even, from_odd = refs[:2]
        del refs[:2]
    outs = refs[:steps]
    del refs[:steps]
    if next_depth:
        to_even, to_odd = refs[:2]
        del refs[:2]
    splits = refs[:steps]
    del refs[:steps]
    if not first:
        halo = refs.pop(0)
    inner = refs
    rows = own.shape[0]
    parity = info[0]
    mask = halves()
    if not first:
        there = info[1] == 1
        for i in range(depth):
            halo[1 - parity, i] = from_even[i]
            tile = from_odd[parity, i]
            halo[parity, i] = jnp.where(there, tile, jnp.zeros_like(tile))
    for i in range(depth):
        splits[0][i] = split(halo[0, i], mask)
        splits[0][depth + rows + i] = split(halo[1, i], mask)
    for i in range(rows):
        splits[0][depth + i] = split(own[i], mask)

    def value(step, row):
        if 0 <= row < rows:
            return own[row] if step == 0 else outs[step - 1][row]
        if step == 0:
            return halo[0, row + depth] if row < 0 else halo[1, row - rows]
        keep = W * (steps - step)
        ref = inner[step - 1]
        return ref[row + keep] if row < 0 else ref[keep + row - rows]

    for step in range(steps):
        keep = W * (steps - 1 - step)
        reach = keep + W
        source = splits[step]
        pairs = list(range(-keep, rows + keep, 2))
        streamed = []
        for row in pairs:
            parts = []
            for k in range(4):
                tiles = [
                    source[offs[(row + h + margin) * 4 + k] + (row + h + reach)] for h in range(2)
                ]
                parts.append(jnp.concatenate(tiles, 0).astype(BF16))
            streamed.append(jnp.concatenate(parts, 1))
        sums = []
        for row, left in zip(pairs, streamed):
            if row < 0:
                mats = halo_high[(row + margin) // 2], halo_low[(row + margin) // 2]
            elif row >= rows:
                at = margin // 2 + (row - rows) // 2
                mats = halo_high[at], halo_low[at]
            else:
                mats = high[row // 2], low[row // 2]
            sums.append(
                jnp.dot(left, mats[0], preferred_element_type=F32)
                + jnp.dot(left, mats[1], preferred_element_type=F32)
            )
        for row, total in zip(pairs, sums):
            for h in range(2):
                at = row + h
                part = total[8 * h : 8 * h + 8, 128 * h : 128 * h + 128]
                part = part + pltpu.roll(part, 4, 0)
                tile = part + (scaled[at + margin] - SCALE * shifts[step]) * value(step, at)
                if 0 <= at < rows:
                    outs[step][at] = tile
                elif at < 0:
                    inner[step][at + keep] = tile
                else:
                    inner[step][keep + at - rows] = tile
                if step < steps - 1:
                    splits[step + 1][at + keep] = split(tile, mask)
    if next_depth:
        last = outs[-1]
        for i in range(next_depth):
            to_even[i] = last[(1 - parity) * (rows - next_depth) + i]
            to_odd[i] = last[parity * (rows - next_depth) + i]


def pair_list():
    half = CHAIN // 2 + 1
    low, top = range(half), range(half, CHAIN + 1)
    return (
        [(i, j) for i in low for j in low if i <= j],
        [(i, j) for i in low for j in top],
        [(i, j) for i in top for j in top if i <= j],
    )


PLACES = {pair: at for at, pair in enumerate(sum(pair_list(), []))}


def dense(ref, p, mask):
    return jnp.where(mask, ref[2 * p], ref[2 * p + 1])


def gram_kernel(*refs):
    vectors, out = refs[:-1], refs[-1]
    count = vectors[0].shape[0] // 2
    mask = halves()
    lane = lax.broadcasted_iota(jnp.int32, (8, 128), 1)
    tile = jnp.zeros((8, 128), F32)
    for pairs in pair_list():
        used = sorted({i for pair in pairs for i in pair})
        total = None
        for p in range(count):
            here = {i: dense(vectors[i], p, mask) for i in used}
            products = [here[i] * here[j] for i, j in pairs]
            total = products if total is None else [a + b for a, b in zip(total, products)]
        for pair, one in zip(pairs, total):
            tile = jnp.where(lane == PLACES[pair], jnp.sum(one, axis=1, keepdims=True), tile)
    for d in range(out.shape[0]):
        out[d] = tile


def small_solve(gram):
    def g(i, j):
        return gram[(i, j) if i <= j else (j, i)]

    right = [[SHIFTS[b] * g(a, b) + GROW * g(a, b + 1) for b in range(S)] for a in range(S + 1)]
    normal = [
        [SHIFTS[a] * right[a][b] + GROW * right[a + 1][b] for b in range(a + 1)] for a in range(S)
    ]
    target = [SHIFTS[a] * g(a, 0) + GROW * g(a + 1, 0) for a in range(S)]
    lower = [[None] * S for _ in range(S)]
    scaled = [[None] * S for _ in range(S)]
    inverse = []
    for j in range(S):
        pivot = normal[j][j]
        for k in range(j):
            pivot = pivot - scaled[j][k] * lower[j][k]
        inverse.append(1.0 / pivot)
        for i in range(j + 1, S):
            entry = normal[i][j]
            for k in range(j):
                entry = entry - scaled[i][k] * lower[j][k]
            scaled[i][j] = entry
            lower[i][j] = entry * inverse[j]
    coeffs = list(target)
    for i in range(S):
        for k in range(i):
            coeffs[i] = coeffs[i] - lower[i][k] * coeffs[k]
    coeffs = [c * d for c, d in zip(coeffs, inverse)]
    for i in reversed(range(S)):
        for k in range(i + 1, S):
            coeffs[i] = coeffs[i] - lower[k][i] * coeffs[k]
    combine = []
    for m in range(S + 1):
        entry = jnp.ones_like(coeffs[0]) if m == 0 else -GROW * coeffs[m - 1]
        if m < S:
            entry = entry - SHIFTS[m] * coeffs[m]
        combine.append(entry)
    return coeffs, combine


def final_kernel(grams, *refs):
    vectors, solution_ref, residual_ref = refs[:-2], refs[-2], refs[-1]
    count = vectors[0].shape[0] // 2
    mask = halves()
    parts = [grams[d] for d in range(grams.shape[0])]
    while len(parts) > 1:
        parts = [a + b for a, b in zip(parts[::2], parts[1::2])] + (
            parts[-1:] if len(parts) % 2 else []
        )
    tile = parts[0] + pltpu.roll(parts[0], 4, 0)
    gram = {
        pair: jnp.broadcast_to(tile[:, at : at + 1], (8, 128)) for pair, at in PLACES.items()
    }

    def g(i, j):
        return gram[(i, j) if i <= j else (j, i)]

    coeffs, combine = small_solve(gram)
    columns = [combine]
    for k in range(S):
        last = columns[-1]
        column = []
        for m in range(len(last) + 1):
            entry = None
            if m < len(last):
                gap = SCALE * (SHIFTS[m % S] - SHIFTS[k])
                entry = gap * last[m] if m % S != k else None
            if m > 0:
                entry = last[m - 1] if entry is None else entry + last[m - 1]
            column.append(jnp.zeros_like(last[0]) if entry is None else entry)
        columns.append(column)
    second = {}
    for b in range(S + 1):
        image = []
        for m in range(len(columns[b])):
            total = None
            for i, c in enumerate(columns[b]):
                term = g(m, i) * c
                total = term if total is None else total + term
            image.append(total)
        for a in range(b + 1):
            total = None
            for m, c in enumerate(columns[a]):
                term = c * image[m]
                total = term if total is None else total + term
            second[(a, b)] = total
    more, ending = small_solve(second)
    to_solution, to_residual = [], []
    for m in range(CHAIN + 1):
        total = coeffs[m] if m < S else None
        for a in range(S):
            if m < len(columns[a]):
                term = more[a] * columns[a][m]
                total = term if total is None else total + term
        to_solution.append(total)
        total = None
        for a in range(S + 1):
            if m < len(columns[a]):
                term = ending[a] * columns[a][m]
                total = term if total is None else total + term
        to_residual.append(total)
    for p in range(count):
        here = [dense(ref, p, mask) for ref in vectors]
        for ref, weights in ((solution_ref, to_solution), (residual_ref, to_residual)):
            total = None
            for weight, one in zip(weights, here):
                if weight is not None:
                    total = weight * one if total is None else total + weight * one
            ref[:, (2 * p) * 128 : (2 * p + 1) * 128] = total[0:4]
            ref[:, (2 * p + 1) * 128 : (2 * p + 2) * 128] = total[4:8]


def shape(*dims, kind=F32):
    return jax.ShapeDtypeStruct(dims, kind)


def local(blocks, offsets, diag_shift, right_side):
    rhs_count = right_side.shape[0]
    rows, per_row, size = blocks.shape[0], blocks.shape[1], blocks.shape[2]
    count, copies = lax.axis_size("dom"), lax.axis_size("groups")
    me = lax.axis_index("dom")
    parity = me % 2
    linked = jnp.logical_and(me > 0, me < count - 1)
    info = jnp.stack([parity, linked.astype(jnp.int32)])
    margin = W * (max(GROUPS) - 1)
    depth = W * GROUPS[0]
    flat = blocks.reshape(rows * per_row * size, size)
    diag = diag_shift.reshape(rows, size)
    message = shape(margin * 512 + 8 * depth + -(-2 * margin // 8) * 8, size)
    start, even, odd = pl.pallas_call(
        functools.partial(prep_kernel, depth, margin),
        out_shape=[shape(rows, 8, size), message, message],
        in_specs=[SM, HB, VM, VM, VM],
        out_specs=[VM] * 3,
        scratch_shapes=[pltpu.SemaphoreType.DMA((2,))],
        compiler_params=params(8),
        name="prepare",
    )(info, flat, right_side, diag, offsets)

    swap_even = [(i, i ^ 1) for i in range(count)]
    swap_odd = [(i, i + 1) for i in range(1, count - 1, 2)]
    swap_odd = swap_odd + [(b, a) for a, b in swap_odd]
    if copies % 2:
        axes, pairs = "dom", [[i, (i + 1) % count] for i in range(1, count, 2)]
    else:
        axes = ("groups", "dom")
        pairs = [[g * count + i, g * count + i + 1] for g in range(copies) for i in range(1, count - 1, 2)]
        for g in range(0, copies, 2):
            pairs += [[g * count + e, (g + 1) * count + e] for e in (0, count - 1)]

    odd = lax.ppermute(odd, "dom", swap_odd)
    even = lax.ppermute(even, "dom", swap_even)

    pair_shape = shape(rows // 2, per_row * size, 2 * size, kind=BF16)
    high, low = pl.pallas_call(
        functools.partial(convert_kernel, 4),
        out_shape=[pair_shape] * 2,
        in_specs=[HB],
        out_specs=[VM] * 2,
        scratch_shapes=[pltpu.VMEM((4, per_row * size, size), F32), pltpu.SemaphoreType.DMA((4,))],
        compiler_params=params(16),
        name="convert",
    )(flat)

    halo_shape = shape(margin, per_row * size, 2 * size, kind=BF16)
    halo_high, halo_low, scaled, halo = pl.pallas_call(
        functools.partial(halo_kernel, depth, margin),
        out_shape=[halo_shape, halo_shape, shape(rows + 2 * margin, 1, size), shape(2, depth, 8, size)],
        in_specs=[SM] + [VM] * 3,
        out_specs=[VM] * 4,
        compiler_params=params(8),
        name="halo",
    )(info, even, odd, diag)

    at = margin * 512 + 8 * depth + margin
    even_offs, odd_offs = even[at : at + margin, :per_row], odd[at : at + margin, :per_row]
    left = jnp.where(parity == 0, odd_offs, even_offs).astype(jnp.int32)
    right = jnp.where(parity == 0, even_offs, odd_offs).astype(jnp.int32)
    all_offs = jnp.concatenate([left, offsets, right], 0).reshape(-1)

    vectors = [start]
    done = 0
    for number, steps in enumerate(GROUPS):
        first = number == 0
        next_depth = W * GROUPS[number + 1] if number + 1 < len(GROUPS) else 0
        depth = W * steps
        outs = [shape(rows, 8, size)] * steps + [shape(next_depth, 8, size)] * (2 if next_depth else 0)
        scratch = [pltpu.VMEM((rows + 2 * W * (steps - j), 8, size), F32) for j in range(steps)]
        if not first:
            scratch.append(pltpu.VMEM((2, depth, 8, size), F32))
        scratch += [pltpu.VMEM((2 * W * (steps - 1 - j), 8, size), F32) for j in range(steps - 1)]
        received = [halo] if first else [even, odd]
        results = pl.pallas_call(
            functools.partial(
                steps_kernel, first, steps, [SHIFTS[(done + j) % S] for j in range(steps)], margin, next_depth
            ),
            out_shape=outs,
            in_specs=[SM, SM] + [VM] * (6 + len(received)),
            out_specs=[VM] * len(outs),
            scratch_shapes=scratch,
            compiler_params=params(16),
            name="steps",
        )(info, all_offs, high, low, halo_high, halo_low, scaled, vectors[-1], *received)
        vectors += results[:steps]
        done += steps
        if next_depth:
            even, odd = results[steps:]
            even = lax.ppermute(even, "dom", swap_even)
            odd = lax.all_gather(odd, axes, axis_index_groups=pairs)

    gram = pl.pallas_call(
        gram_kernel,
        out_shape=shape(count, 8, size),
        in_specs=[VM] * len(vectors),
        out_specs=VM,
        compiler_params=params(16),
        name="gram",
    )(*vectors)
    gram = lax.all_to_all(gram, "dom", 0, 0)
    return tuple(
        pl.pallas_call(
            final_kernel,
            out_shape=[shape(rhs_count, rows * size)] * 2,
            in_specs=[VM] * (1 + len(vectors)),
            out_specs=[VM] * 2,
            compiler_params=params(16),
            name="finish",
        )(gram, *vectors)
    )


def solution(mesh):
    in_specs = (
        P(("groups", "dom"), None, None, None),
        P(("groups", "dom"), None),
        P(("groups", "dom")),
        P(None, ("groups", "dom")),
    )
    out_specs = (P(None, ("groups", "dom")), P(None, ("groups", "dom")))
    return jax.shard_map(local, mesh=mesh, in_specs=in_specs, out_specs=out_specs, check_vma=False)
```

```python
import functools
import math

import jax
import jax.numpy as jnp
import numpy as np
from jax import lax
from jax.experimental import pallas as pl
from jax.experimental.pallas import tpu as pltpu
from jax.sharding import PartitionSpec as P

W = 2
S = 6
CYCLES = 2
CHAIN = S * CYCLES
GROUPS = (2, 2, 2, 2, 2, 2)
SCALE = 0.125
GROW = 1.0 / SCALE
SHIFTS = [
    float(np.float32(1.6) + np.float32(0.8) * np.float32(math.cos(math.pi * (2 * j + 1) / (2 * S))))
    for j in range(S)
]
F32 = jnp.float32
BF16 = jnp.bfloat16
VM = pl.BlockSpec(memory_space=pltpu.VMEM)
SM = pl.BlockSpec(memory_space=pltpu.SMEM)
HB = pl.BlockSpec(memory_space=pltpu.HBM)


def params(mib):
    return pltpu.CompilerParams(vmem_limit_bytes=mib << 20)


def halves():
    return lax.broadcasted_iota(jnp.int32, (8, 128), 0) < 4


def split(tile, mask):
    high = tile.astype(BF16).astype(F32)
    return jnp.where(mask, high, tile - high)


def store_pair(block, high_ref, low_ref, pair, half, k):
    turned = block.T * SCALE
    high = turned.astype(BF16)
    low = (turned - high.astype(F32)).astype(BF16)
    rows, cols = slice(k * 128, (k + 1) * 128), slice(half * 128, (half + 1) * 128)
    high_ref[pair, rows, cols] = high
    low_ref[pair, rows, cols] = low


def prep_kernel(depth, margin, info, blocks, rhs, diag, offs, start, scaled, even, odd, rhs_buf, diag_buf, offs_buf, sems):
    rows = diag.shape[0]
    parity = info[0]
    sides = ((even, 1 - parity), (odd, parity))
    copies = [
        pltpu.make_async_copy(rhs, rhs_buf, sems.at[0]),
        pltpu.make_async_copy(diag, diag_buf, sems.at[1]),
        pltpu.make_async_copy(offs, offs_buf, sems.at[2]),
    ]
    for place, (ref, at) in enumerate(sides):
        first = pl.multiple_of(at * (rows - margin) * 512, 512)
        copies.append(
            pltpu.make_async_copy(
                blocks.at[pl.ds(first, margin * 512)],
                ref.at[pl.ds(0, margin * 512)],
                sems.at[3 + place],
            )
        )
    for copy in copies:
        copy.start()
    for copy in copies[:3]:
        copy.wait()
    for i in range(rows):
        part = rhs_buf[:, i * 128 : (i + 1) * 128]
        start[i] = jnp.concatenate([part, part], 0)
        scaled[i] = diag_buf[i : i + 1, :] * SCALE
    places = offs_buf[...].astype(F32)
    places = jnp.concatenate([places, jnp.zeros((4, 128 - rows), F32)], 1)
    for ref, at in sides:
        base = margin * 512
        for i in range(depth):
            ref[base + 8 * i : base + 8 * i + 8, :] = start[at * (rows - depth) + i]
        base += 8 * depth
        ref[base : base + 4, :] = places
        own = jnp.where(at == 1, diag_buf[rows - margin :, :], diag_buf[:margin, :])
        ref[base + 4 : base + 4 + margin, :] = own
        if margin < 4:
            ref[base + 4 + margin : base + 8, :] = jnp.zeros((4 - margin, 128), F32)
    for copy in copies[3:]:
        copy.wait()


def take_message(depth, margin, rows, parity, even, odd, high, low, scaled, places, halo):
    for ref, side in ((even, 1 - parity), (odd, parity)):
        for m in range(margin):
            for k in range(4):
                first = (m * 4 + k) * 128
                store_pair(
                    ref[first : first + 128, :], high, low, side * (margin // 2) + m // 2, m % 2, k
                )
        base = margin * 512
        for i in range(depth):
            halo[side, i] = ref[base + 8 * i : base + 8 * i + 8, :]
        base += 8 * depth
        for m in range(margin):
            scaled[side * margin + m] = ref[base + 4 + m : base + 5 + m, :] * SCALE
            for k in range(4):
                line = ref[base + k : base + k + 1, :]
                at_left, at_right = rows - margin + m, m
                one = jnp.where(
                    side == 0, line[:, at_left : at_left + 1], line[:, at_right : at_right + 1]
                )
                places[(side * margin + m) * 4 + k] = jnp.broadcast_to(one, (8, 128))


class Chain:
    def __init__(self, rows, margin, steps, shifts, offs, high, low, scaled, halo_parts=None):
        self.rows, self.margin, self.steps, self.shifts = rows, margin, steps, shifts
        self.offs, self.high, self.low, self.scaled = offs, high, low, scaled
        self.halo_parts = halo_parts
        self.mask = halves()

    def halo_at(self, row):
        return row + self.margin if row < 0 else self.margin + row - self.rows

    def mats(self, row):
        if 0 <= row < self.rows:
            return self.high[row // 2], self.low[row // 2]
        at = self.halo_at(row) // 2
        return self.halo_parts[0][at], self.halo_parts[1][at]

    def diagonal(self, row):
        if 0 <= row < self.rows:
            return self.scaled[row]
        return self.halo_parts[2][self.halo_at(row)]

    def gather(self, source, reach, row, k):
        if 0 <= row < self.rows:
            return source[self.offs[k, row] + (row + reach)]
        place = self.halo_parts[3][self.halo_at(row) * 4 + k]
        total = jnp.zeros((8, 128), F32)
        for c in range(-W, W + 1):
            total = jnp.where(place == c, source[row + c + reach], total)
        return total

    def run(self, plan, values, known, splits, store):
        for step in range(self.steps):
            source, reach = splits[step], W * (self.steps - step)
            needed = {row + c for first in plan[step] for row in (first, first + 1) for c in range(-W, W + 1)}
            for row in sorted(needed & set(known[step])):
                source[row + reach] = split(values(step, row), self.mask)
            streamed = []
            for row in plan[step]:
                parts = []
                for k in range(4):
                    tiles = [self.gather(source, reach, row + h, k) for h in range(2)]
                    parts.append(jnp.concatenate(tiles, 0).astype(BF16))
                streamed.append(jnp.concatenate(parts, 1))
            sums = []
            for row, left in zip(plan[step], streamed):
                high, low = self.mats(row)
                sums.append(
                    jnp.dot(left, high, preferred_element_type=F32)
                    + jnp.dot(left, low, preferred_element_type=F32)
                )
            for row, total in zip(plan[step], sums):
                for h in range(2):
                    at = row + h
                    part = total[8 * h : 8 * h + 8, 128 * h : 128 * h + 128]
                    part = part + pltpu.roll(part, 4, 0)
                    tile = part + (self.diagonal(at) - SCALE * self.shifts[step]) * values(step, at)
                    store(step, at, tile)
                    if step < self.steps - 1:
                        splits[step + 1][at + reach - W] = split(tile, self.mask)


def inner_plan(rows, steps):
    return [list(range(W * (j + 1), rows - W * (j + 1), 2)) for j in range(steps)]


def whole_plan(rows, steps):
    return [list(range(-W * (steps - 1 - j), rows + W * (steps - 1 - j), 2)) for j in range(steps)]


def convert_kernel(slots, steps, shifts, *refs):
    offs, blocks, scaled, start, high, low = refs[:6]
    outs, splits = refs[6 : 6 + steps], refs[6 + steps : 6 + 2 * steps]
    buf, sems = refs[6 + 2 * steps :]
    rows = blocks.shape[0] // 512

    def fetch(i, slot):
        first = pl.multiple_of(i * 512, 512)
        return pltpu.make_async_copy(blocks.at[pl.ds(first, 512)], buf.at[slot], sems.at[slot])

    for slot in range(slots):
        fetch(slot, slot).start()

    def body(q, carry):
        for slot in range(slots):
            i = q * slots + slot
            fetch(i, slot).wait()
            for k in range(4):
                store_pair(
                    buf[slot, k * 128 : (k + 1) * 128, :],
                    high,
                    low,
                    q * (slots // 2) + slot // 2,
                    slot % 2,
                    k,
                )

            @pl.when(i + slots < rows)
            def _():
                fetch(i + slots, slot).start()

        return carry

    lax.fori_loop(0, rows // slots, body, 0)
    chain = Chain(rows, 0, steps, shifts, offs, high, low, scaled)
    plan = inner_plan(rows, steps)

    def values(step, row):
        return start[row] if step == 0 else outs[step - 1][row]

    def store(step, row, tile):
        outs[step][row] = tile

    chain.run(plan, values, [range(rows)] + [[]] * (steps - 1), splits, store)


def send(parity, last, depth, to_even, to_odd):
    rows = last.shape[0]
    for i in range(depth):
        to_even[i] = last[(1 - parity) * (rows - depth) + i]
        to_odd[i] = last[parity * (rows - depth) + i]


def first_kernel(steps, shifts, margin, next_depth, *refs):
    refs = list(refs)
    info, offs, even, odd, high, low, scaled, own = refs[:8]
    del refs[:8]
    begun, outs = refs[:steps], refs[steps + 4 : 2 * steps + 4]
    parts = refs[steps : steps + 4]
    del refs[: 2 * steps + 4]
    to_even, to_odd = refs[:2]
    splits, halo, inner = refs[2 : 2 + steps], refs[2 + steps], refs[3 + steps :]
    rows = own.shape[0]
    parity = info[0]
    take_message(W * steps, margin, rows, parity, even, odd, *parts, halo)
    chain = Chain(rows, margin, steps, shifts, offs, high, low, scaled, parts)
    before, whole = inner_plan(rows, steps), whole_plan(rows, steps)
    plan = [[row for row in w if row not in b] for b, w in zip(before, whole)]
    done = [[row + h for row in b for h in range(2)] for b in before]
    for j in range(steps):
        for row in done[j]:
            outs[j][row] = begun[j][row]
    values, store = vector_access(rows, steps, own, outs, halo, inner)
    known = [range(-W * steps, rows + W * steps)] + done[:-1]
    chain.run(plan, values, known, splits, store)
    send(parity, outs[-1], next_depth, to_even, to_odd)


def vector_access(rows, steps, own, outs, halo, inner):
    depth = W * steps

    def values(step, row):
        if 0 <= row < rows:
            return own[row] if step == 0 else outs[step - 1][row]
        if step == 0:
            return halo[0, row + depth] if row < 0 else halo[1, row - rows]
        keep = W * (steps - step)
        return inner[step - 1][row + keep if row < 0 else keep + row - rows]

    def store(step, row, tile):
        if 0 <= row < rows:
            outs[step][row] = tile
        else:
            keep = W * (steps - 1 - step)
            inner[step][row + keep if row < 0 else keep + row - rows] = tile

    return values, store


def steps_kernel(steps, shifts, margin, next_depth, *refs):
    refs = list(refs)
    info, offs, high, low, scaled, own = refs[:6]
    parts = refs[6:10]
    from_even, from_odd = refs[10:12]
    del refs[:12]
    outs = refs[:steps]
    del refs[:steps]
    if next_depth:
        to_even, to_odd = refs[:2]
        del refs[:2]
    splits, halo, inner = refs[:steps], refs[steps], refs[steps + 1 :]
    rows = own.shape[0]
    depth = W * steps
    parity, there = info[0], info[1] == 1
    for i in range(depth):
        halo[1 - parity, i] = from_even[i]
        tile = from_odd[parity, i]
        halo[parity, i] = jnp.where(there, tile, jnp.zeros_like(tile))
    chain = Chain(rows, margin, steps, shifts, offs, high, low, scaled, parts)
    values, store = vector_access(rows, steps, own, outs, halo, inner)
    known = [range(-depth, rows + depth)] + [[]] * (steps - 1)
    chain.run(whole_plan(rows, steps), values, known, splits, store)
    if next_depth:
        send(parity, outs[-1], next_depth, to_even, to_odd)


def pair_list():
    half = CHAIN // 2 + 1
    low, top = range(half), range(half, CHAIN + 1)
    return (
        [(i, j) for i in low for j in low if i <= j],
        [(i, j) for i in low for j in top],
        [(i, j) for i in top for j in top if i <= j],
    )


PLACES = {pair: at for at, pair in enumerate(sum(pair_list(), []))}


def dense(ref, p, mask):
    return jnp.where(mask, ref[2 * p], ref[2 * p + 1])


def gram_kernel(*refs):
    vectors, out = refs[:-1], refs[-1]
    count = vectors[0].shape[0] // 2
    mask = halves()
    lane = lax.broadcasted_iota(jnp.int32, (8, 128), 1)
    tile = jnp.zeros((8, 128), F32)
    for pairs in pair_list():
        used = sorted({i for pair in pairs for i in pair})
        total = None
        for p in range(count):
            here = {i: dense(vectors[i], p, mask) for i in used}
            products = [here[i] * here[j] for i, j in pairs]
            total = products if total is None else [a + b for a, b in zip(total, products)]
        for pair, one in zip(pairs, total):
            tile = jnp.where(lane == PLACES[pair], jnp.sum(one, axis=1, keepdims=True), tile)
    for d in range(out.shape[0]):
        out[d] = tile


def small_solve(gram):
    def g(i, j):
        return gram[(i, j) if i <= j else (j, i)]

    right = [[SHIFTS[b] * g(a, b) + GROW * g(a, b + 1) for b in range(S)] for a in range(S + 1)]
    normal = [
        [SHIFTS[a] * right[a][b] + GROW * right[a + 1][b] for b in range(a + 1)] for a in range(S)
    ]
    target = [SHIFTS[a] * g(a, 0) + GROW * g(a + 1, 0) for a in range(S)]
    lower = [[None] * S for _ in range(S)]
    scaled = [[None] * S for _ in range(S)]
    inverse = []
    for j in range(S):
        pivot = normal[j][j]
        for k in range(j):
            pivot = pivot - scaled[j][k] * lower[j][k]
        inverse.append(1.0 / pivot)
        for i in range(j + 1, S):
            entry = normal[i][j]
            for k in range(j):
                entry = entry - scaled[i][k] * lower[j][k]
            scaled[i][j] = entry
            lower[i][j] = entry * inverse[j]
    coeffs = list(target)
    for i in range(S):
        for k in range(i):
            coeffs[i] = coeffs[i] - lower[i][k] * coeffs[k]
    coeffs = [c * d for c, d in zip(coeffs, inverse)]
    for i in reversed(range(S)):
        for k in range(i + 1, S):
            coeffs[i] = coeffs[i] - lower[k][i] * coeffs[k]
    combine = []
    for m in range(S + 1):
        entry = jnp.ones_like(coeffs[0]) if m == 0 else -GROW * coeffs[m - 1]
        if m < S:
            entry = entry - SHIFTS[m] * coeffs[m]
        combine.append(entry)
    return coeffs, combine


def final_kernel(grams, *refs):
    vectors, solution_ref, residual_ref = refs[:-2], refs[-2], refs[-1]
    count = vectors[0].shape[0] // 2
    mask = halves()
    parts = [grams[d] for d in range(grams.shape[0])]
    while len(parts) > 1:
        parts = [a + b for a, b in zip(parts[::2], parts[1::2])] + (
            parts[-1:] if len(parts) % 2 else []
        )
    tile = parts[0] + pltpu.roll(parts[0], 4, 0)
    gram = {
        pair: jnp.broadcast_to(tile[:, at : at + 1], (8, 128)) for pair, at in PLACES.items()
    }

    def g(i, j):
        return gram[(i, j) if i <= j else (j, i)]

    coeffs, combine = small_solve(gram)
    columns = [combine]
    for k in range(S):
        last = columns[-1]
        column = []
        for m in range(len(last) + 1):
            entry = None
            if m < len(last):
                gap = SCALE * (SHIFTS[m % S] - SHIFTS[k])
                entry = gap * last[m] if m % S != k else None
            if m > 0:
                entry = last[m - 1] if entry is None else entry + last[m - 1]
            column.append(jnp.zeros_like(last[0]) if entry is None else entry)
        columns.append(column)
    second = {}
    for b in range(S + 1):
        image = []
        for m in range(len(columns[b])):
            total = None
            for i, c in enumerate(columns[b]):
                term = g(m, i) * c
                total = term if total is None else total + term
            image.append(total)
        for a in range(b + 1):
            total = None
            for m, c in enumerate(columns[a]):
                term = c * image[m]
                total = term if total is None else total + term
            second[(a, b)] = total
    more, ending = small_solve(second)
    to_solution, to_residual = [], []
    for m in range(CHAIN + 1):
        total = coeffs[m] if m < S else None
        for a in range(S):
            if m < len(columns[a]):
                term = more[a] * columns[a][m]
                total = term if total is None else total + term
        to_solution.append(total)
        total = None
        for a in range(S + 1):
            if m < len(columns[a]):
                term = ending[a] * columns[a][m]
                total = term if total is None else total + term
        to_residual.append(total)
    for p in range(count):
        here = [dense(ref, p, mask) for ref in vectors]
        for ref, weights in ((solution_ref, to_solution), (residual_ref, to_residual)):
            total = None
            for weight, one in zip(weights, here):
                if weight is not None:
                    total = weight * one if total is None else total + weight * one
            ref[:, (2 * p) * 128 : (2 * p + 1) * 128] = total[0:4]
            ref[:, (2 * p + 1) * 128 : (2 * p + 2) * 128] = total[4:8]


def shape(*dims, kind=F32):
    return jax.ShapeDtypeStruct(dims, kind)


def local(blocks, offsets, diag_shift, right_side):
    rhs_count = right_side.shape[0]
    rows, per_row, size = blocks.shape[0], blocks.shape[1], blocks.shape[2]
    count, copies = lax.axis_size("dom"), lax.axis_size("groups")
    me = lax.axis_index("dom")
    parity = me % 2
    linked = jnp.logical_and(me > 0, me < count - 1)
    info = jnp.stack([parity, linked.astype(jnp.int32)])
    margin = W * (max(GROUPS) - 1)
    steps = GROUPS[0]
    depth, next_depth = W * steps, W * GROUPS[1]
    flat = pltpu.with_memory_space_constraint(blocks.reshape(rows * per_row * size, size), pltpu.HBM)
    offs = offsets.T
    diag = diag_shift.reshape(rows, size)
    message = shape(margin * 512 + 8 * depth + 8, size)
    start, scaled, even, odd = pl.pallas_call(
        functools.partial(prep_kernel, depth, margin),
        out_shape=[shape(rows, 8, size), shape(rows, 1, size), message, message],
        in_specs=[SM, HB, HB, HB, HB],
        out_specs=[VM] * 4,
        scratch_shapes=[
            pltpu.VMEM(right_side.shape, F32),
            pltpu.VMEM(diag.shape, F32),
            pltpu.VMEM(offs.shape, jnp.int32),
            pltpu.SemaphoreType.DMA((5,)),
        ],
        compiler_params=params(8),
        name="prepare",
    )(
        info,
        flat,
        *[pltpu.with_memory_space_constraint(x, pltpu.HBM) for x in (right_side, diag, offs)],
    )

    swap_even = [(i, i ^ 1) for i in range(count)]
    swap_odd = [(i, i + 1) for i in range(1, count - 1, 2)]
    swap_odd = swap_odd + [(b, a) for a, b in swap_odd]
    if copies % 2:
        axes, pairs = "dom", [[i, (i + 1) % count] for i in range(1, count, 2)]
    else:
        axes = ("groups", "dom")
        pairs = [[g * count + i, g * count + i + 1] for g in range(copies) for i in range(1, count - 1, 2)]
        for g in range(0, copies, 2):
            pairs += [[g * count + e, (g + 1) * count + e] for e in (0, count - 1)]

    odd = lax.ppermute(odd, "dom", swap_odd)
    even = lax.ppermute(even, "dom", swap_even)

    vector = shape(rows, 8, size)
    pair_shape = pltpu.VMEM((rows // 2, per_row * size, 2 * size), BF16)
    split_scratch = [pltpu.VMEM((rows + 2 * W * (steps - j), 8, size), F32) for j in range(steps)]
    high, low, *begun = pl.pallas_call(
        functools.partial(convert_kernel, 4, steps, SHIFTS[:steps]),
        out_shape=[pair_shape] * 2 + [vector] * steps,
        in_specs=[SM, HB, VM, VM],
        out_specs=[VM] * (2 + steps),
        scratch_shapes=split_scratch
        + [pltpu.VMEM((4, per_row * size, size), F32), pltpu.SemaphoreType.DMA((4,))],
        compiler_params=params(16),
        name="convert",
    )(offs, flat, scaled, start)

    halo_shape = pltpu.VMEM((margin, per_row * size, 2 * size), BF16)
    results = pl.pallas_call(
        functools.partial(first_kernel, steps, SHIFTS[:steps], margin, next_depth),
        out_shape=[halo_shape, halo_shape, shape(2 * margin, 1, size), shape(8 * margin, 8, size)]
        + [vector] * steps
        + [shape(next_depth, 8, size)] * 2,
        in_specs=[SM, SM] + [VM] * (6 + steps),
        out_specs=[VM] * (6 + steps),
        scratch_shapes=split_scratch
        + [pltpu.VMEM((2, depth, 8, size), F32)]
        + [pltpu.VMEM((2 * W * (steps - 1 - j), 8, size), F32) for j in range(steps - 1)],
        compiler_params=params(16),
        name="first",
    )(info, offs, even, odd, high, low, scaled, start, *begun)
    parts = results[:4]
    vectors = [start, *results[4 : 4 + steps]]
    even, odd = results[4 + steps :]
    done = steps
    for number, steps in enumerate(GROUPS[1:], 1):
        even = lax.ppermute(even, "dom", swap_even)
        odd = lax.all_gather(odd, axes, axis_index_groups=pairs)
        next_depth = W * GROUPS[number + 1] if number + 1 < len(GROUPS) else 0
        outs = [vector] * steps + [shape(next_depth, 8, size)] * (2 if next_depth else 0)
        results = pl.pallas_call(
            functools.partial(
                steps_kernel, steps, [SHIFTS[(done + j) % S] for j in range(steps)], margin, next_depth
            ),
            out_shape=outs,
            in_specs=[SM, SM] + [VM] * 10,
            out_specs=[VM] * len(outs),
            scratch_shapes=[pltpu.VMEM((rows + 2 * W * (steps - j), 8, size), F32) for j in range(steps)]
            + [pltpu.VMEM((2, W * steps, 8, size), F32)]
            + [pltpu.VMEM((2 * W * (steps - 1 - j), 8, size), F32) for j in range(steps - 1)],
            compiler_params=params(16),
            name="steps",
        )(info, offs, high, low, scaled, vectors[-1], *parts, even, odd)
        vectors += results[:steps]
        done += steps
        if next_depth:
            even, odd = results[steps:]

    gram = pl.pallas_call(
        gram_kernel,
        out_shape=shape(count, 8, size),
        in_specs=[VM] * len(vectors),
        out_specs=VM,
        compiler_params=params(16),
        name="gram",
    )(*vectors)
    gram = lax.all_to_all(gram, "dom", 0, 0)
    return tuple(
        pl.pallas_call(
            final_kernel,
            out_shape=[shape(rhs_count, rows * size)] * 2,
            in_specs=[VM] * (1 + len(vectors)),
            out_specs=[VM] * 2,
            compiler_params=params(16),
            name="finish",
        )(gram, *vectors)
    )


def solution(mesh):
    in_specs = (
        P(("groups", "dom"), None, None, None),
        P(("groups", "dom"), None),
        P(("groups", "dom")),
        P(None, ("groups", "dom")),
    )
    out_specs = (P(None, ("groups", "dom")), P(None, ("groups", "dom")))
    return jax.shard_map(local, mesh=mesh, in_specs=in_specs, out_specs=out_specs, check_vma=False)
```

```python
import functools
import math

import jax
import jax.numpy as jnp
import numpy as np
from jax import lax
from jax.experimental import pallas as pl
from jax.experimental.pallas import tpu as pltpu
from jax.sharding import PartitionSpec as P

W = 2
S = 6
CYCLES = 2
CHAIN = S * CYCLES
GROUPS = (2, 2, 2, 2, 2, 2)
AHEAD = 4
INNER_SECOND = False
SCALE = 0.125
GROW = 1.0 / SCALE
SHIFTS = [
    float(np.float32(1.6) + np.float32(0.8) * np.float32(math.cos(math.pi * (2 * j + 1) / (2 * S))))
    for j in range(S)
]
F32 = jnp.float32
BF16 = jnp.bfloat16
VM = pl.BlockSpec(memory_space=pltpu.VMEM)
SM = pl.BlockSpec(memory_space=pltpu.SMEM)
HB = pl.BlockSpec(memory_space=pltpu.HBM)


def params(mib):
    return pltpu.CompilerParams(vmem_limit_bytes=mib << 20)


def halves():
    return lax.broadcasted_iota(jnp.int32, (8, 128), 0) < 4


def split(tile, mask):
    high = tile.astype(BF16).astype(F32)
    return jnp.where(mask, high, tile - high)


def store_pair(block, high_ref, low_ref, pair, half, k):
    block = block * SCALE
    high = block.astype(BF16)
    low = (block - high.astype(F32)).astype(BF16)
    rows, cols = slice(k * 128, (k + 1) * 128), slice(half * 128, (half + 1) * 128)
    high_ref[pair, rows, cols] = high.T
    low_ref[pair, rows, cols] = low.T


def prep_kernel(depth, margin, info, blocks, rhs, diag, offs, even, odd, rhs_buf, diag_buf, offs_buf, sems):
    rows = diag.shape[0]
    parity = info[0]
    sides = ((even, 1 - parity), (odd, parity))
    copies = [
        pltpu.make_async_copy(rhs, rhs_buf, sems.at[0]),
        pltpu.make_async_copy(diag, diag_buf, sems.at[1]),
        pltpu.make_async_copy(offs, offs_buf, sems.at[2]),
    ]
    for place, (ref, at) in enumerate(sides):
        first = pl.multiple_of(at * (rows - margin) * 512, 512)
        copies.append(
            pltpu.make_async_copy(
                blocks.at[pl.ds(first, margin * 512)],
                ref.at[pl.ds(0, margin * 512)],
                sems.at[3 + place],
            )
        )
    for copy in copies:
        copy.start()
    for copy in copies[:3]:
        copy.wait()
    places = offs_buf[...].astype(F32)
    places = jnp.concatenate([places, jnp.zeros((4, 128 - rows), F32)], 1)
    for ref, at in sides:
        base = margin * 512
        for i in range(depth):
            low, top = i * 128, (rows - depth + i) * 128
            part = jnp.where(at == 1, rhs_buf[:, top : top + 128], rhs_buf[:, low : low + 128])
            ref[base + 8 * i : base + 8 * i + 8, :] = jnp.concatenate([part, part], 0)
        base += 8 * depth
        ref[base : base + 4, :] = places
        own = jnp.where(at == 1, diag_buf[rows - margin :, :], diag_buf[:margin, :])
        ref[base + 4 : base + 4 + margin, :] = own
        if margin < 4:
            ref[base + 4 + margin : base + 8, :] = jnp.zeros((4 - margin, 128), F32)
    for copy in copies[3:]:
        copy.wait()


def take_message(depth, margin, rows, parity, even, odd, high, low, scaled, places, halo):
    for ref, side in ((even, 1 - parity), (odd, parity)):
        for m in range(margin):
            for k in range(4):
                first = (m * 4 + k) * 128
                store_pair(
                    ref[first : first + 128, :], high, low, side * (margin // 2) + m // 2, m % 2, k
                )
        base = margin * 512
        for i in range(depth):
            halo[side, i] = ref[base + 8 * i : base + 8 * i + 8, :]
        base += 8 * depth
        for m in range(margin):
            scaled[side * margin + m] = ref[base + 4 + m : base + 5 + m, :] * SCALE
            for k in range(4):
                line = ref[base + k : base + k + 1, :]
                at_left, at_right = rows - margin + m, m
                one = jnp.where(
                    side == 0, line[:, at_left : at_left + 1], line[:, at_right : at_right + 1]
                )
                places[(side * margin + m) * 4 + k] = jnp.broadcast_to(one, (8, 128))


class Chain:
    def __init__(self, rows, margin, steps, shifts, offs, high, low, scaled, halo_parts=None):
        self.rows, self.margin, self.steps, self.shifts = rows, margin, steps, shifts
        self.offs, self.high, self.low, self.scaled = offs, high, low, scaled
        self.halo_parts = halo_parts
        self.mask = halves()

    def halo_at(self, row):
        return row + self.margin if row < 0 else self.margin + row - self.rows

    def mats(self, row):
        if 0 <= row < self.rows:
            return self.high[row // 2], self.low[row // 2]
        at = self.halo_at(row) // 2
        return self.halo_parts[0][at], self.halo_parts[1][at]

    def diagonal(self, row):
        if 0 <= row < self.rows:
            return self.scaled[row]
        return self.halo_parts[2][self.halo_at(row)]

    def gather(self, source, reach, row, k):
        if 0 <= row < self.rows:
            return source[self.offs[k, row] + (row + reach)]
        place = self.halo_parts[3][self.halo_at(row) * 4 + k]
        total = jnp.zeros((8, 128), F32)
        for c in range(-W, W + 1):
            total = jnp.where(place == c, source[row + c + reach], total)
        return total

    def run(self, plan, values, known, splits, store):
        for step in range(self.steps):
            source, reach = splits[step], W * (self.steps - step)
            needed = {row + c for first in plan[step] for row in (first, first + 1) for c in range(-W, W + 1)}
            for row in sorted(needed & set(known[step])):
                source[row + reach] = split(values(step, row), self.mask)
            streamed = []
            for row in plan[step]:
                parts = []
                for k in range(4):
                    tiles = [self.gather(source, reach, row + h, k) for h in range(2)]
                    parts.append(jnp.concatenate(tiles, 0).astype(BF16))
                streamed.append(jnp.concatenate(parts, 1))
            sums = []
            for row, left in zip(plan[step], streamed):
                high, low = self.mats(row)
                sums.append(
                    jnp.dot(left, high, preferred_element_type=F32)
                    + jnp.dot(left, low, preferred_element_type=F32)
                )
            for row, total in zip(plan[step], sums):
                for h in range(2):
                    at = row + h
                    part = total[8 * h : 8 * h + 8, 128 * h : 128 * h + 128]
                    part = part + pltpu.roll(part, 4, 0)
                    tile = part + (self.diagonal(at) - SCALE * self.shifts[step]) * values(step, at)
                    store(step, at, tile)
                    if step < self.steps - 1:
                        splits[step + 1][at + reach - W] = split(tile, self.mask)


def inner_rows(rows, step):
    return list(range(W * step, rows - W * step)) if rows > 2 * W * step else []


def without(rows, done):
    return [row for row in rows[::2] if row not in set(done)]


def whole_rows(rows, steps, step):
    return list(range(-W * (steps - step), rows + W * (steps - step)))


def copy_rows(begun, outs, done):
    for old, new, rows in zip(begun, outs, done):
        for row in rows:
            new[row] = old[row]


def vector_access(rows, steps, own, outs, halo=None, inner=None):
    depth = W * steps

    def values(step, row):
        if 0 <= row < rows:
            return own[row] if step == 0 else outs[step - 1][row]
        if step == 0:
            return halo[0, row + depth] if row < 0 else halo[1, row - rows]
        keep = W * (steps - step)
        return inner[step - 1][row + keep if row < 0 else keep + row - rows]

    def store(step, row, tile):
        if 0 <= row < rows:
            outs[step][row] = tile
        else:
            keep = W * (steps - 1 - step)
            inner[step][row + keep if row < 0 else keep + row - rows] = tile

    return values, store


def convert_kernel(steps, shifts, *refs):
    offs, blocks, rhs, diag, start, scaled, high, low = refs[:8]
    outs, splits = refs[8 : 8 + steps], refs[8 + steps : 8 + 2 * steps]
    buf, sems = refs[8 + 2 * steps :]
    rows = buf.shape[0]

    def fetch(i):
        first = pl.multiple_of(i * 512, 512)
        return pltpu.make_async_copy(blocks.at[pl.ds(first, 512)], buf.at[i], sems.at[i])

    for i in range(rows):
        fetch(i).start()
    for i in range(rows):
        part = rhs[:, i * 128 : (i + 1) * 128]
        start[i] = jnp.concatenate([part, part], 0)
        scaled[i] = diag[i : i + 1, :] * SCALE

    def body(p, carry):
        for half in range(2):
            i = 2 * p + half
            fetch(i).wait()
            for k in range(4):
                store_pair(buf[i, k * 128 : (k + 1) * 128, :], high, low, p, half, k)
        return carry

    lax.fori_loop(0, rows // 2, body, 0)
    chain = Chain(rows, 0, steps, shifts, offs, high, low, scaled)
    plan = [without(inner_rows(rows, j + 1), []) for j in range(steps)]
    values, store = vector_access(rows, steps, start, outs)
    chain.run(plan, values, [range(rows)] + [[]] * (steps - 1), splits, store)


def inner_kernel(steps, shifts, done, *refs):
    offs, high, low, scaled, own = refs[:5]
    begun = refs[5 : 5 + len(done)]
    outs = refs[5 + len(done) : 5 + len(done) + steps]
    splits = refs[5 + len(done) + steps :]
    rows = own.shape[0]
    copy_rows(begun, outs, done)
    done = list(done) + [[]] * (steps - len(done))
    chain = Chain(rows, 0, steps, shifts, offs, high, low, scaled)
    plan = [without(inner_rows(rows, j + 1), done[j]) for j in range(steps)]
    values, store = vector_access(rows, steps, own, outs)
    chain.run(plan, values, [range(rows)] + done[:-1], splits, store)


def rest_kernel(first, steps, shifts, margin, done, next_depth, *refs):
    refs = list(refs)
    info, offs, high, low, scaled, own, from_even, from_odd = refs[:8]
    del refs[:8]
    begun = refs[:steps]
    del refs[:steps]
    parts = refs[:4]
    del refs[:4]
    outs = refs[:steps]
    del refs[:steps]
    if next_depth:
        to_even, to_odd = refs[:2]
        del refs[:2]
    splits, halo, inner = refs[:steps], refs[steps], refs[steps + 1 :]
    rows = own.shape[0]
    depth = W * steps
    parity = info[0]
    if first:
        take_message(depth, margin, rows, parity, from_even, from_odd, *parts, halo)
    else:
        for i in range(depth):
            halo[1 - parity, i] = from_even[i]
            halo[parity, i] = from_odd[i]
    copy_rows(begun, outs, done)
    chain = Chain(rows, margin, steps, shifts, offs, high, low, scaled, parts)
    plan = [without(whole_rows(rows, steps, j + 1), done[j]) for j in range(steps)]
    values, store = vector_access(rows, steps, own, outs, halo, inner)
    known = [range(-depth, rows + depth)] + list(done[:-1])
    chain.run(plan, values, known, splits, store)
    if next_depth:
        last = outs[-1]
        for i in range(next_depth):
            to_even[i] = last[(1 - parity) * (rows - next_depth) + i]
            to_odd[i] = last[parity * (rows - next_depth) + i]


def pair_list():
    half = CHAIN // 2 + 1
    low, top = range(half), range(half, CHAIN + 1)
    return (
        [(i, j) for i in low for j in low if i <= j],
        [(i, j) for i in low for j in top],
        [(i, j) for i in top for j in top if i <= j],
    )


PLACES = {pair: at for at, pair in enumerate(sum(pair_list(), []))}


def dense(ref, p, mask):
    return jnp.where(mask, ref[2 * p], ref[2 * p + 1])


def gram_kernel(*refs):
    vectors, out = refs[:-1], refs[-1]
    count = vectors[0].shape[0] // 2
    mask = halves()
    lane = lax.broadcasted_iota(jnp.int32, (8, 128), 1)
    tile = jnp.zeros((8, 128), F32)
    for pairs in pair_list():
        used = sorted({i for pair in pairs for i in pair})
        total = None
        for p in range(count):
            here = {i: dense(vectors[i], p, mask) for i in used}
            products = [here[i] * here[j] for i, j in pairs]
            total = products if total is None else [a + b for a, b in zip(total, products)]
        for pair, one in zip(pairs, total):
            tile = jnp.where(lane == PLACES[pair], jnp.sum(one, axis=1, keepdims=True), tile)
    out[...] = tile + pltpu.roll(tile, 4, 0)


def small_solve(gram):
    def g(i, j):
        return gram[(i, j) if i <= j else (j, i)]

    right = [[SHIFTS[b] * g(a, b) + GROW * g(a, b + 1) for b in range(S)] for a in range(S + 1)]
    normal = [
        [SHIFTS[a] * right[a][b] + GROW * right[a + 1][b] for b in range(a + 1)] for a in range(S)
    ]
    target = [SHIFTS[a] * g(a, 0) + GROW * g(a + 1, 0) for a in range(S)]
    lower = [[None] * S for _ in range(S)]
    scaled = [[None] * S for _ in range(S)]
    inverse = []
    for j in range(S):
        pivot = normal[j][j]
        for k in range(j):
            pivot = pivot - scaled[j][k] * lower[j][k]
        inverse.append(1.0 / pivot)
        for i in range(j + 1, S):
            entry = normal[i][j]
            for k in range(j):
                entry = entry - scaled[i][k] * lower[j][k]
            scaled[i][j] = entry
            lower[i][j] = entry * inverse[j]
    coeffs = list(target)
    for i in range(S):
        for k in range(i):
            coeffs[i] = coeffs[i] - lower[i][k] * coeffs[k]
    coeffs = [c * d for c, d in zip(coeffs, inverse)]
    for i in reversed(range(S)):
        for k in range(i + 1, S):
            coeffs[i] = coeffs[i] - lower[k][i] * coeffs[k]
    combine = []
    for m in range(S + 1):
        entry = jnp.ones_like(coeffs[0]) if m == 0 else -GROW * coeffs[m - 1]
        if m < S:
            entry = entry - SHIFTS[m] * coeffs[m]
        combine.append(entry)
    return coeffs, combine


def final_kernel(total_gram, *refs):
    vectors, solution_ref, residual_ref = refs[:-2], refs[-2], refs[-1]
    count = vectors[0].shape[0] // 2
    mask = halves()
    tile = total_gram[...]
    gram = {
        pair: jnp.broadcast_to(tile[:, at : at + 1], (8, 128)) for pair, at in PLACES.items()
    }

    def g(i, j):
        return gram[(i, j) if i <= j else (j, i)]

    coeffs, combine = small_solve(gram)
    columns = [combine]
    for k in range(S):
        last = columns[-1]
        column = []
        for m in range(len(last) + 1):
            entry = None
            if m < len(last):
                gap = SCALE * (SHIFTS[m % S] - SHIFTS[k])
                entry = gap * last[m] if m % S != k else None
            if m > 0:
                entry = last[m - 1] if entry is None else entry + last[m - 1]
            column.append(jnp.zeros_like(last[0]) if entry is None else entry)
        columns.append(column)
    second = {}
    for b in range(S + 1):
        image = []
        for m in range(len(columns[b])):
            total = None
            for i, c in enumerate(columns[b]):
                term = g(m, i) * c
                total = term if total is None else total + term
            image.append(total)
        for a in range(b + 1):
            total = None
            for m, c in enumerate(columns[a]):
                term = c * image[m]
                total = term if total is None else total + term
            second[(a, b)] = total
    more, ending = small_solve(second)
    to_solution, to_residual = [], []
    for m in range(CHAIN + 1):
        total = coeffs[m] if m < S else None
        for a in range(S):
            if m < len(columns[a]):
                term = more[a] * columns[a][m]
                total = term if total is None else total + term
        to_solution.append(total)
        total = None
        for a in range(S + 1):
            if m < len(columns[a]):
                term = ending[a] * columns[a][m]
                total = term if total is None else total + term
        to_residual.append(total)
    for p in range(count):
        here = [dense(ref, p, mask) for ref in vectors]
        for ref, weights in ((solution_ref, to_solution), (residual_ref, to_residual)):
            total = None
            for weight, one in zip(weights, here):
                if weight is not None:
                    total = weight * one if total is None else total + weight * one
            ref[:, (2 * p) * 128 : (2 * p + 1) * 128] = total[0:4]
            ref[:, (2 * p + 1) * 128 : (2 * p + 2) * 128] = total[4:8]


def shape(*dims, kind=F32):
    return jax.ShapeDtypeStruct(dims, kind)


def cost(block_rows):
    return pl.CostEstimate(flops=block_rows * 2**21, bytes_accessed=block_rows * 2**18, transcendentals=0)


def local(blocks, offsets, diag_shift, right_side):
    rhs_count = right_side.shape[0]
    rows, per_row, size = blocks.shape[0], blocks.shape[1], blocks.shape[2]
    count = lax.axis_size("dom")
    info = (lax.axis_index("dom") % 2).reshape(1)
    margin = W * (max(GROUPS) - 1)
    steps = GROUPS[0]
    depth = W * steps
    flat = pltpu.with_memory_space_constraint(blocks.reshape(rows * per_row * size, size), pltpu.HBM)
    offs = offsets.T
    diag = diag_shift.reshape(rows, size)
    message = shape(margin * 512 + 8 * depth + 8, size)
    even, odd = pl.pallas_call(
        functools.partial(prep_kernel, depth, margin),
        out_shape=[message, message],
        in_specs=[SM, HB, HB, HB, HB],
        out_specs=[VM] * 2,
        scratch_shapes=[
            pltpu.VMEM(right_side.shape, F32),
            pltpu.VMEM(diag.shape, F32),
            pltpu.VMEM(offs.shape, jnp.int32),
            pltpu.SemaphoreType.DMA((5,)),
        ],
        compiler_params=params(8),
        name="prepare",
    )(
        info,
        flat,
        *[pltpu.with_memory_space_constraint(x, pltpu.HBM) for x in (right_side, diag, offs)],
    )

    swap_even = [(i, i ^ 1) for i in range(count)]
    swap_odd = [(i, i + 1) for i in range(1, count - 1, 2)]
    swap_odd = swap_odd + [(b, a) for a, b in swap_odd]

    def exchange(even, odd):
        odd = lax.ppermute(odd, "dom", swap_odd)
        return lax.ppermute(even, "dom", swap_even), odd

    even, odd = exchange(even, odd)

    vector = shape(rows, 8, size)
    pair_shape = pltpu.VMEM((rows // 2, per_row * size, 2 * size), BF16)

    def buffers(steps):
        return [pltpu.VMEM((rows + 2 * W * (steps - j), 8, size), F32) for j in range(steps)]

    started = [inner_rows(rows, j + 1) for j in range(AHEAD)]
    start, scaled, high, low, *ahead = pl.pallas_call(
        functools.partial(convert_kernel, AHEAD, [SHIFTS[j % S] for j in range(AHEAD)]),
        out_shape=[vector, shape(rows, 1, size)] + [pair_shape] * 2 + [vector] * AHEAD,
        in_specs=[SM, HB, VM, VM],
        out_specs=[VM] * (4 + AHEAD),
        scratch_shapes=buffers(AHEAD)
        + [pltpu.VMEM((rows, per_row * size, size), F32), pltpu.SemaphoreType.DMA((rows,))],
        compiler_params=params(24),
        cost_estimate=cost(2 * rows + sum(len(r) for r in started)),
        name="convert",
    )(offs, flat, right_side, diag)

    vectors = [start]
    halo_shape = pltpu.VMEM((margin, per_row * size, 2 * size), BF16)
    parts = None
    at = 0
    for number, steps in enumerate(GROUPS):
        shifts = [SHIFTS[(at + j) % S] for j in range(steps)]
        depth = W * steps
        begun, done = ahead[at : at + steps], started[at : at + steps]
        inner = [inner_rows(rows, j + 1) for j in range(steps)]
        if done != inner and (number > 1 or INNER_SECOND or not begun):
            begun = pl.pallas_call(
                functools.partial(inner_kernel, steps, shifts, done),
                out_shape=[vector] * steps,
                in_specs=[SM] + [VM] * (4 + len(begun)),
                out_specs=[VM] * steps,
                scratch_shapes=buffers(steps),
                compiler_params=params(16),
                cost_estimate=cost(sum(len(r) for r in inner)),
                name="inner",
            )(offs, high, low, scaled, vectors[-1], *begun)
            done = inner
        next_depth = W * GROUPS[number + 1] if number + 1 < len(GROUPS) else 0
        first = number == 0
        outs = [vector] * steps + [shape(next_depth, 8, size)] * (2 if next_depth else 0)
        if first:
            outs = [halo_shape, halo_shape, shape(2 * margin, 1, size), shape(8 * margin, 8, size)] + outs
        results = pl.pallas_call(
            functools.partial(rest_kernel, first, steps, shifts, margin, done, next_depth),
            out_shape=outs,
            in_specs=[SM, SM] + [VM] * (6 + steps + (0 if first else 4)),
            out_specs=[VM] * len(outs),
            scratch_shapes=buffers(steps)
            + [pltpu.VMEM((2, depth, 8, size), F32)]
            + [pltpu.VMEM((2 * W * (steps - 1 - j), 8, size), F32) for j in range(steps - 1)],
            compiler_params=params(16),
            cost_estimate=cost(16),
            name="rest",
        )(info, offs, high, low, scaled, vectors[-1], even, odd, *begun, *(parts or []))
        results = list(results)
        if first:
            parts, results = results[:4], results[4:]
        vectors += results[:steps]
        at += steps
        if next_depth:
            even, odd = exchange(*results[steps:])

    gram = pl.pallas_call(
        gram_kernel,
        out_shape=shape(8, size),
        in_specs=[VM] * len(vectors),
        out_specs=VM,
        compiler_params=params(16),
        name="gram",
    )(*vectors)
    if count & (count - 1):
        gram = lax.psum(gram, "dom")
    else:
        for stage in range(count.bit_length() - 1):
            gram = gram + lax.ppermute(gram, "dom", [(i, i ^ (1 << stage)) for i in range(count)])
    return tuple(
        pl.pallas_call(
            final_kernel,
            out_shape=[shape(rhs_count, rows * size)] * 2,
            in_specs=[VM] * (1 + len(vectors)),
            out_specs=[VM] * 2,
            compiler_params=params(16),
            name="finish",
        )(gram, *vectors)
    )


def solution(mesh):
    in_specs = (
        P(("groups", "dom"), None, None, None),
        P(("groups", "dom"), None),
        P(("groups", "dom")),
        P(None, ("groups", "dom")),
    )
    out_specs = (P(None, ("groups", "dom")), P(None, ("groups", "dom")))
    return jax.shard_map(local, mesh=mesh, in_specs=in_specs, out_specs=out_specs, check_vma=False)
```

```python
import functools
import math

import jax
import jax.numpy as jnp
import numpy as np
from jax import lax
from jax.experimental import pallas as pl
from jax.experimental.pallas import tpu as pltpu
from jax.sharding import PartitionSpec as P

W = 2
S = 6
CYCLES = 2
CHAIN = S * CYCLES
GROUPS = (2, 2, 2, 2, 2, 2)
AHEAD = 4
INNER_SECOND = False
SCALE = 0.125
GROW = 1.0 / SCALE
SHIFTS = [
    float(np.float32(1.6) + np.float32(0.8) * np.float32(math.cos(math.pi * (2 * j + 1) / (2 * S))))
    for j in range(S)
]
F32 = jnp.float32
BF16 = jnp.bfloat16
VM = pl.BlockSpec(memory_space=pltpu.VMEM)
HB = pl.BlockSpec(memory_space=pltpu.HBM)


def params(mib):
    return pltpu.CompilerParams(vmem_limit_bytes=mib << 20)


def halves():
    return lax.broadcasted_iota(jnp.int32, (8, 128), 0) < 4


def split(tile, mask):
    high = tile.astype(BF16).astype(F32)
    return jnp.where(mask, high, tile - high)


def store_pair(block, high_ref, low_ref, pair, half, k):
    block = block * SCALE
    high = block.astype(BF16)
    low = (block - high.astype(F32)).astype(BF16)
    rows, cols = slice(k * 128, (k + 1) * 128), slice(half * 128, (half + 1) * 128)
    high_ref[pair, rows, cols] = high.T
    low_ref[pair, rows, cols] = low.T


def prep_kernel(depth, margin, blocks, rhs, diag, offs, even, odd, rhs_buf, diag_buf, offs_buf, sems):
    rows = diag.shape[0]
    parity = lax.axis_index("dom") % 2
    sides = ((even, 1 - parity), (odd, parity))
    copies = [
        pltpu.make_async_copy(rhs, rhs_buf, sems.at[0]),
        pltpu.make_async_copy(diag, diag_buf, sems.at[1]),
        pltpu.make_async_copy(offs, offs_buf, sems.at[2]),
    ]
    for place, (ref, at) in enumerate(sides):
        first = pl.multiple_of(at * (rows - margin) * 512, 512)
        copies.append(
            pltpu.make_async_copy(
                blocks.at[pl.ds(first, margin * 512)],
                ref.at[pl.ds(0, margin * 512)],
                sems.at[3 + place],
            )
        )
    for copy in copies:
        copy.start()
    for copy in copies[:3]:
        copy.wait()
    places = offs_buf[...].astype(F32)
    places = jnp.concatenate([places, jnp.zeros((4, 128 - rows), F32)], 1)
    for ref, at in sides:
        base = margin * 512
        for i in range(depth):
            low, top = i * 128, (rows - depth + i) * 128
            part = jnp.where(at == 1, rhs_buf[:, top : top + 128], rhs_buf[:, low : low + 128])
            ref[base + 8 * i : base + 8 * i + 8, :] = jnp.concatenate([part, part], 0)
        base += 8 * depth
        ref[base : base + 4, :] = places
        own = jnp.where(at == 1, diag_buf[rows - margin :, :], diag_buf[:margin, :])
        ref[base + 4 : base + 4 + margin, :] = own
        if margin < 4:
            ref[base + 4 + margin : base + 8, :] = jnp.zeros((4 - margin, 128), F32)
    for copy in copies[3:]:
        copy.wait()


def take_message(depth, margin, rows, parity, even, odd, high, low, scaled, places, halo):
    for ref, side in ((even, 1 - parity), (odd, parity)):
        for m in range(margin):
            for k in range(4):
                first = (m * 4 + k) * 128
                store_pair(
                    ref[first : first + 128, :], high, low, side * (margin // 2) + m // 2, m % 2, k
                )
        base = margin * 512
        for i in range(depth):
            halo[side, i] = ref[base + 8 * i : base + 8 * i + 8, :]
        base += 8 * depth
        for m in range(margin):
            scaled[side * margin + m] = ref[base + 4 + m : base + 5 + m, :] * SCALE
            for k in range(1, 4):
                line = ref[base + k : base + k + 1, :]
                at_left, at_right = rows - margin + m, m
                one = jnp.where(
                    side == 0, line[:, at_left : at_left + 1], line[:, at_right : at_right + 1]
                )
                places[k - 1, side * margin + m] = jnp.broadcast_to(one, (1, 128))


class Chain:
    def __init__(self, rows, margin, steps, shifts, places, high, low, scaled, halo_parts=None):
        self.rows, self.margin, self.steps, self.shifts = rows, margin, steps, shifts
        self.places, self.high, self.low, self.scaled = places, high, low, scaled
        self.halo_parts = halo_parts
        self.mask = halves()

    def halo_at(self, row):
        return row + self.margin if row < 0 else self.margin + row - self.rows

    def mats(self, row):
        if 0 <= row < self.rows:
            return self.high[row // 2], self.low[row // 2]
        at = self.halo_at(row) // 2
        return self.halo_parts[0][at], self.halo_parts[1][at]

    def diagonal(self, row):
        if 0 <= row < self.rows:
            return self.scaled[row]
        return self.halo_parts[2][self.halo_at(row)]

    def gather(self, source, reach, row, k):
        if k == 0:
            return source[row + reach]
        if 0 <= row < self.rows:
            place = self.places[k - 1, row]
        else:
            place = self.halo_parts[3][k - 1, self.halo_at(row)]
        place = jnp.broadcast_to(place, (8, 128))
        total = source[row + W + reach]
        for c in (-W, 1 - W, W - 1):
            total = jnp.where(place == c, source[row + c + reach], total)
        return total

    def run(self, plan, values, known, splits, store):
        for step in range(self.steps):
            source, reach = splits[step], W * (self.steps - step)
            needed = {row + c for first in plan[step] for row in (first, first + 1) for c in range(-W, W + 1)}
            for row in sorted(needed & set(known[step])):
                source[row + reach] = split(values(step, row), self.mask)
            streamed = []
            for row in plan[step]:
                parts = []
                for k in range(4):
                    tiles = [self.gather(source, reach, row + h, k) for h in range(2)]
                    parts.append(jnp.concatenate(tiles, 0).astype(BF16))
                streamed.append(jnp.concatenate(parts, 1))
            sums = []
            for row, left in zip(plan[step], streamed):
                high, low = self.mats(row)
                sums.append(
                    jnp.dot(left, high, preferred_element_type=F32)
                    + jnp.dot(left, low, preferred_element_type=F32)
                )
            for row, total in zip(plan[step], sums):
                for h in range(2):
                    at = row + h
                    part = total[8 * h : 8 * h + 8, 128 * h : 128 * h + 128]
                    part = part + pltpu.roll(part, 4, 0)
                    tile = part + (self.diagonal(at) - SCALE * self.shifts[step]) * values(step, at)
                    store(step, at, tile)
                    if step < self.steps - 1:
                        splits[step + 1][at + reach - W] = split(tile, self.mask)


def inner_rows(rows, step):
    return list(range(W * step, rows - W * step)) if rows > 2 * W * step else []


def without(rows, done):
    return [row for row in rows[::2] if row not in set(done)]


def whole_rows(rows, steps, step):
    return list(range(-W * (steps - step), rows + W * (steps - step)))


def copy_rows(begun, outs, done):
    for old, new, rows in zip(begun, outs, done):
        for row in rows:
            new[row] = old[row]


def vector_access(rows, steps, own, outs, halo=None, inner=None):
    depth = W * steps

    def values(step, row):
        if 0 <= row < rows:
            return own[row] if step == 0 else outs[step - 1][row]
        if step == 0:
            return halo[0, row + depth] if row < 0 else halo[1, row - rows]
        keep = W * (steps - step)
        return inner[step - 1][row + keep if row < 0 else keep + row - rows]

    def store(step, row, tile):
        if 0 <= row < rows:
            outs[step][row] = tile
        else:
            keep = W * (steps - 1 - step)
            inner[step][row + keep if row < 0 else keep + row - rows] = tile

    return values, store


def convert_kernel(steps, shifts, *refs):
    blocks, rhs, diag, offs, start, scaled, places, high, low = refs[:9]
    outs, splits = refs[9 : 9 + steps], refs[9 + steps : 9 + 2 * steps]
    buf, sems = refs[9 + 2 * steps :]
    rows = buf.shape[0]

    def fetch(i):
        first = pl.multiple_of(i * 512, 512)
        return pltpu.make_async_copy(blocks.at[pl.ds(first, 512)], buf.at[i], sems.at[i])

    for i in range(rows):
        fetch(i).start()
    for i in range(rows):
        part = rhs[:, i * 128 : (i + 1) * 128]
        start[i] = jnp.concatenate([part, part], 0)
        scaled[i] = diag[i : i + 1, :] * SCALE
    turned = jnp.concatenate([offs[...].astype(F32), jnp.zeros((4, 128 - rows), F32)], 1)
    turned = jnp.concatenate([turned, jnp.zeros((4, 128), F32)], 0).T
    for k in range(1, 4):
        places[k - 1] = jnp.broadcast_to(turned[:rows, k : k + 1], (rows, 128)).reshape(rows, 1, 128)

    def body(p, carry):
        for half in range(2):
            i = 2 * p + half
            fetch(i).wait()
            for k in range(4):
                store_pair(buf[i, k * 128 : (k + 1) * 128, :], high, low, p, half, k)
        return carry

    lax.fori_loop(0, rows // 2, body, 0)
    chain = Chain(rows, 0, steps, shifts, places, high, low, scaled)
    plan = [without(inner_rows(rows, j + 1), []) for j in range(steps)]
    values, store = vector_access(rows, steps, start, outs)
    chain.run(plan, values, [range(rows)] + [[]] * (steps - 1), splits, store)


def inner_kernel(steps, shifts, done, *refs):
    places, high, low, scaled, own = refs[:5]
    begun = refs[5 : 5 + len(done)]
    outs = refs[5 + len(done) : 5 + len(done) + steps]
    splits = refs[5 + len(done) + steps :]
    rows = own.shape[0]
    copy_rows(begun, outs, done)
    done = list(done) + [[]] * (steps - len(done))
    chain = Chain(rows, 0, steps, shifts, places, high, low, scaled)
    plan = [without(inner_rows(rows, j + 1), done[j]) for j in range(steps)]
    values, store = vector_access(rows, steps, own, outs)
    chain.run(plan, values, [range(rows)] + done[:-1], splits, store)


def rest_kernel(first, steps, shifts, margin, done, next_depth, *refs):
    refs = list(refs)
    places, high, low, scaled, own, from_even, from_odd = refs[:7]
    del refs[:7]
    begun = refs[:steps]
    del refs[:steps]
    parts = refs[:4]
    del refs[:4]
    outs = refs[:steps]
    del refs[:steps]
    if next_depth:
        to_even, to_odd = refs[:2]
        del refs[:2]
    splits, halo, inner = refs[:steps], refs[steps], refs[steps + 1 :]
    rows = own.shape[0]
    depth = W * steps
    parity = lax.axis_index("dom") % 2
    if first:
        take_message(depth, margin, rows, parity, from_even, from_odd, *parts, halo)
    else:
        for i in range(depth):
            halo[1 - parity, i] = from_even[i]
            halo[parity, i] = from_odd[i]
    copy_rows(begun, outs, done)
    chain = Chain(rows, margin, steps, shifts, places, high, low, scaled, parts)
    plan = [without(whole_rows(rows, steps, j + 1), done[j]) for j in range(steps)]
    values, store = vector_access(rows, steps, own, outs, halo, inner)
    known = [range(-depth, rows + depth)] + list(done[:-1])
    chain.run(plan, values, known, splits, store)
    if next_depth:
        last = outs[-1]
        for i in range(next_depth):
            to_even[i] = last[(1 - parity) * (rows - next_depth) + i]
            to_odd[i] = last[parity * (rows - next_depth) + i]


def pair_list():
    half = CHAIN // 2 + 1
    low, top = range(half), range(half, CHAIN + 1)
    return (
        [(i, j) for i in low for j in low if i <= j],
        [(i, j) for i in low for j in top],
        [(i, j) for i in top for j in top if i <= j],
    )


PLACES = {pair: at for at, pair in enumerate(sum(pair_list(), []))}


def dense(ref, p, mask):
    return jnp.where(mask, ref[2 * p], ref[2 * p + 1])


def gram_kernel(*refs):
    vectors, out = refs[:-1], refs[-1]
    count = vectors[0].shape[0] // 2
    mask = halves()
    lane = lax.broadcasted_iota(jnp.int32, (8, 128), 1)
    tile = jnp.zeros((8, 128), F32)
    for pairs in pair_list():
        used = sorted({i for pair in pairs for i in pair})
        total = None
        for p in range(count):
            here = {i: dense(vectors[i], p, mask) for i in used}
            products = [here[i] * here[j] for i, j in pairs]
            total = products if total is None else [a + b for a, b in zip(total, products)]
        for pair, one in zip(pairs, total):
            tile = jnp.where(lane == PLACES[pair], jnp.sum(one, axis=1, keepdims=True), tile)
    out[...] = tile + pltpu.roll(tile, 4, 0)


def small_solve(gram):
    def g(i, j):
        return gram[(i, j) if i <= j else (j, i)]

    right = [[SHIFTS[b] * g(a, b) + GROW * g(a, b + 1) for b in range(S)] for a in range(S + 1)]
    normal = [
        [SHIFTS[a] * right[a][b] + GROW * right[a + 1][b] for b in range(a + 1)] for a in range(S)
    ]
    target = [SHIFTS[a] * g(a, 0) + GROW * g(a + 1, 0) for a in range(S)]
    lower = [[None] * S for _ in range(S)]
    scaled = [[None] * S for _ in range(S)]
    inverse = []
    for j in range(S):
        pivot = normal[j][j]
        for k in range(j):
            pivot = pivot - scaled[j][k] * lower[j][k]
        inverse.append(1.0 / pivot)
        for i in range(j + 1, S):
            entry = normal[i][j]
            for k in range(j):
                entry = entry - scaled[i][k] * lower[j][k]
            scaled[i][j] = entry
            lower[i][j] = entry * inverse[j]
    coeffs = list(target)
    for i in range(S):
        for k in range(i):
            coeffs[i] = coeffs[i] - lower[i][k] * coeffs[k]
    coeffs = [c * d for c, d in zip(coeffs, inverse)]
    for i in reversed(range(S)):
        for k in range(i + 1, S):
            coeffs[i] = coeffs[i] - lower[k][i] * coeffs[k]
    combine = []
    for m in range(S + 1):
        entry = jnp.ones_like(coeffs[0]) if m == 0 else -GROW * coeffs[m - 1]
        if m < S:
            entry = entry - SHIFTS[m] * coeffs[m]
        combine.append(entry)
    return coeffs, combine


def final_kernel(total_gram, *refs):
    vectors, solution_ref, residual_ref = refs[:-2], refs[-2], refs[-1]
    count = vectors[0].shape[0] // 2
    mask = halves()
    tile = total_gram[...]
    gram = {
        pair: jnp.broadcast_to(tile[:, at : at + 1], (8, 128)) for pair, at in PLACES.items()
    }

    def g(i, j):
        return gram[(i, j) if i <= j else (j, i)]

    coeffs, combine = small_solve(gram)
    columns = [combine]
    for k in range(S):
        last = columns[-1]
        column = []
        for m in range(len(last) + 1):
            entry = None
            if m < len(last):
                gap = SCALE * (SHIFTS[m % S] - SHIFTS[k])
                entry = gap * last[m] if m % S != k else None
            if m > 0:
                entry = last[m - 1] if entry is None else entry + last[m - 1]
            column.append(jnp.zeros_like(last[0]) if entry is None else entry)
        columns.append(column)
    second = {}
    for b in range(S + 1):
        image = []
        for m in range(len(columns[b])):
            total = None
            for i, c in enumerate(columns[b]):
                term = g(m, i) * c
                total = term if total is None else total + term
            image.append(total)
        for a in range(b + 1):
            total = None
            for m, c in enumerate(columns[a]):
                term = c * image[m]
                total = term if total is None else total + term
            second[(a, b)] = total
    more, ending = small_solve(second)
    to_solution, to_residual = [], []
    for m in range(CHAIN + 1):
        total = coeffs[m] if m < S else None
        for a in range(S):
            if m < len(columns[a]):
                term = more[a] * columns[a][m]
                total = term if total is None else total + term
        to_solution.append(total)
        total = None
        for a in range(S + 1):
            if m < len(columns[a]):
                term = ending[a] * columns[a][m]
                total = term if total is None else total + term
        to_residual.append(total)
    for p in range(count):
        here = [dense(ref, p, mask) for ref in vectors]
        for ref, weights in ((solution_ref, to_solution), (residual_ref, to_residual)):
            total = None
            for weight, one in zip(weights, here):
                if weight is not None:
                    total = weight * one if total is None else total + weight * one
            ref[:, (2 * p) * 128 : (2 * p + 1) * 128] = total[0:4]
            ref[:, (2 * p + 1) * 128 : (2 * p + 2) * 128] = total[4:8]


def shape(*dims, kind=F32):
    return jax.ShapeDtypeStruct(dims, kind)


def cost(block_rows):
    return pl.CostEstimate(flops=block_rows * 2**21, bytes_accessed=block_rows * 2**18, transcendentals=0)


def local(blocks, offsets, diag_shift, right_side):
    rhs_count = right_side.shape[0]
    rows, per_row, size = blocks.shape[0], blocks.shape[1], blocks.shape[2]
    count = lax.axis_size("dom")
    margin = W * (max(GROUPS) - 1)
    steps = GROUPS[0]
    depth = W * steps
    flat = pltpu.with_memory_space_constraint(blocks.reshape(rows * per_row * size, size), pltpu.HBM)
    offs = offsets.T
    diag = diag_shift.reshape(rows, size)
    message = shape(margin * 512 + 8 * depth + 8, size)
    even, odd = pl.pallas_call(
        functools.partial(prep_kernel, depth, margin),
        out_shape=[message, message],
        in_specs=[HB, HB, HB, HB],
        out_specs=[VM] * 2,
        scratch_shapes=[
            pltpu.VMEM(right_side.shape, F32),
            pltpu.VMEM(diag.shape, F32),
            pltpu.VMEM(offs.shape, jnp.int32),
            pltpu.SemaphoreType.DMA((5,)),
        ],
        compiler_params=params(8),
        name="prepare",
    )(
        flat,
        *[pltpu.with_memory_space_constraint(x, pltpu.HBM) for x in (right_side, diag, offs)],
    )

    swap_even = [(i, i ^ 1) for i in range(count)]
    swap_odd = [(i, i + 1) for i in range(1, count - 1, 2)]
    swap_odd = swap_odd + [(b, a) for a, b in swap_odd]

    def exchange(even, odd):
        odd = lax.ppermute(odd, "dom", swap_odd)
        return lax.ppermute(even, "dom", swap_even), odd

    even, odd = exchange(even, odd)

    vector = shape(rows, 8, size)
    pair_shape = pltpu.VMEM((rows // 2, per_row * size, 2 * size), BF16)

    def buffers(steps):
        return [pltpu.VMEM((rows + 2 * W * (steps - j), 8, size), F32) for j in range(steps)]

    started = [inner_rows(rows, j + 1) for j in range(AHEAD)]
    start, scaled, places, high, low, *ahead = pl.pallas_call(
        functools.partial(convert_kernel, AHEAD, [SHIFTS[j % S] for j in range(AHEAD)]),
        out_shape=[vector, shape(rows, 1, size), shape(per_row - 1, rows, 1, size)]
        + [pair_shape] * 2
        + [vector] * AHEAD,
        in_specs=[HB, VM, VM, VM],
        out_specs=[VM] * (5 + AHEAD),
        scratch_shapes=buffers(AHEAD)
        + [pltpu.VMEM((rows, per_row * size, size), F32), pltpu.SemaphoreType.DMA((rows,))],
        compiler_params=params(24),
        cost_estimate=cost(2 * rows + sum(len(r) for r in started)),
        name="convert",
    )(flat, right_side, diag, offs)

    vectors = [start]
    halo_shape = pltpu.VMEM((margin, per_row * size, 2 * size), BF16)
    parts = None
    at = 0
    for number, steps in enumerate(GROUPS):
        shifts = [SHIFTS[(at + j) % S] for j in range(steps)]
        depth = W * steps
        begun, done = ahead[at : at + steps], started[at : at + steps]
        inner = [inner_rows(rows, j + 1) for j in range(steps)]
        if done != inner and (number > 1 or INNER_SECOND or not begun):
            begun = pl.pallas_call(
                functools.partial(inner_kernel, steps, shifts, done),
                out_shape=[vector] * steps,
                in_specs=[VM] * (5 + len(begun)),
                out_specs=[VM] * steps,
                scratch_shapes=buffers(steps),
                compiler_params=params(16),
                cost_estimate=cost(sum(len(r) for r in inner)),
                name="inner",
            )(places, high, low, scaled, vectors[-1], *begun)
            done = inner
        next_depth = W * GROUPS[number + 1] if number + 1 < len(GROUPS) else 0
        first = number == 0
        outs = [vector] * steps + [shape(next_depth, 8, size)] * (2 if next_depth else 0)
        if first:
            outs = [halo_shape, halo_shape, shape(2 * margin, 1, size), shape(per_row - 1, 2 * margin, 1, size)] + outs
        results = pl.pallas_call(
            functools.partial(rest_kernel, first, steps, shifts, margin, done, next_depth),
            out_shape=outs,
            in_specs=[VM] * (7 + steps + (0 if first else 4)),
            out_specs=[VM] * len(outs),
            scratch_shapes=buffers(steps)
            + [pltpu.VMEM((2, depth, 8, size), F32)]
            + [pltpu.VMEM((2 * W * (steps - 1 - j), 8, size), F32) for j in range(steps - 1)],
            compiler_params=params(16),
            cost_estimate=cost(16),
            name="rest",
        )(places, high, low, scaled, vectors[-1], even, odd, *begun, *(parts or []))
        results = list(results)
        if first:
            parts, results = results[:4], results[4:]
        vectors += results[:steps]
        at += steps
        if next_depth:
            even, odd = exchange(*results[steps:])

    gram = pl.pallas_call(
        gram_kernel,
        out_shape=shape(8, size),
        in_specs=[VM] * len(vectors),
        out_specs=VM,
        compiler_params=params(16),
        name="gram",
    )(*vectors)
    if count & (count - 1):
        gram = lax.psum(gram, "dom")
    else:
        for stage in range(count.bit_length() - 1):
            gram = gram + lax.ppermute(gram, "dom", [(i, i ^ (1 << stage)) for i in range(count)])
    return tuple(
        pl.pallas_call(
            final_kernel,
            out_shape=[shape(rhs_count, rows * size)] * 2,
            in_specs=[VM] * (1 + len(vectors)),
            out_specs=[VM] * 2,
            compiler_params=params(16),
            name="finish",
        )(gram, *vectors)
    )


def solution(mesh):
    in_specs = (
        P(("groups", "dom"), None, None, None),
        P(("groups", "dom"), None),
        P(("groups", "dom")),
        P(None, ("groups", "dom")),
    )
    out_specs = (P(None, ("groups", "dom")), P(None, ("groups", "dom")))
    return jax.shard_map(local, mesh=mesh, in_specs=in_specs, out_specs=out_specs, check_vma=False)
```

```python
import functools
import math

import jax
import jax.numpy as jnp
import numpy as np
from jax import lax
from jax.experimental import pallas as pl
from jax.experimental.pallas import tpu as pltpu
from jax.sharding import PartitionSpec as P

W = 2
S = 6
CYCLES = 2
CHAIN = S * CYCLES
GROUPS = (2, 2, 2, 2, 2, 2)
AHEAD = 4
INNER_SECOND = True
SCALE = 0.125
GROW = 1.0 / SCALE
SHIFTS = [
    float(np.float32(1.6) + np.float32(0.8) * np.float32(math.cos(math.pi * (2 * j + 1) / (2 * S))))
    for j in range(S)
]
F32 = jnp.float32
BF16 = jnp.bfloat16
VM = pl.BlockSpec(memory_space=pltpu.VMEM)
HB = pl.BlockSpec(memory_space=pltpu.HBM)


def params(mib):
    return pltpu.CompilerParams(vmem_limit_bytes=mib << 20)


def halves():
    return lax.broadcasted_iota(jnp.int32, (8, 128), 0) < 4


def split(tile, mask):
    high = tile.astype(BF16).astype(F32)
    return jnp.where(mask, high, tile - high)


def store_pair(block, high_ref, low_ref, pair, half, k, factor=SCALE):
    block = block * factor
    high = block.astype(BF16)
    low = (block - high.astype(F32)).astype(BF16)
    rows, cols = slice(k * 128, (k + 1) * 128), slice(half * 128, (half + 1) * 128)
    high_ref[pair, rows, cols] = high.T
    low_ref[pair, rows, cols] = low.T


def prep_kernel(depth, margin, blocks, rhs, diag, offs, even, odd, rhs_buf, diag_buf, offs_buf, sems):
    rows = diag.shape[0]
    parity = lax.axis_index("dom") % 2
    sides = ((even, 1 - parity), (odd, parity))
    copies = [
        pltpu.make_async_copy(rhs, rhs_buf, sems.at[0]),
        pltpu.make_async_copy(diag, diag_buf, sems.at[1]),
        pltpu.make_async_copy(offs, offs_buf, sems.at[2]),
    ]
    for place, (ref, at) in enumerate(sides):
        first = pl.multiple_of(at * (rows - margin) * 512, 512)
        copies.append(
            pltpu.make_async_copy(
                blocks.at[pl.ds(first, margin * 512)],
                ref.at[pl.ds(0, margin * 512)],
                sems.at[3 + place],
            )
        )
    for copy in copies:
        copy.start()
    for copy in copies[:3]:
        copy.wait()
    places = offs_buf[...].astype(F32)
    places = jnp.concatenate([places, jnp.zeros((4, 128 - rows), F32)], 1)
    for ref, at in sides:
        base = margin * 512
        for i in range(depth):
            low, top = i * 128, (rows - depth + i) * 128
            part = jnp.where(at == 1, rhs_buf[:, top : top + 128], rhs_buf[:, low : low + 128])
            ref[base + 8 * i : base + 8 * i + 8, :] = jnp.concatenate([part, part], 0)
        base += 8 * depth
        ref[base : base + 4, :] = places
        own = jnp.where(at == 1, diag_buf[rows - margin :, :], diag_buf[:margin, :])
        ref[base + 4 : base + 4 + margin, :] = own
        if margin < 4:
            ref[base + 4 + margin : base + 8, :] = jnp.zeros((4 - margin, 128), F32)
    for copy in copies[3:]:
        copy.wait()


def at_inside():
    me = lax.axis_index("dom")
    return jnp.logical_and(me > 0, me < lax.axis_size("dom") - 1)


def take_vectors(depth, parity, even, odd, halo):
    inside = at_inside()
    for i in range(depth):
        halo[1 - parity, i] = even(i)
        tile = odd(i)
        halo[parity, i] = jnp.where(inside, tile, jnp.zeros_like(tile))


def take_message(depth, margin, rows, parity, even, odd, high, low, scaled, places, halo):
    base = margin * 512
    take_vectors(
        depth,
        parity,
        lambda i: even[base + 8 * i : base + 8 * i + 8, :],
        lambda i: odd[base + 8 * i : base + 8 * i + 8, :],
        halo,
    )
    factor = jnp.where(at_inside(), SCALE, 0.0)
    for ref, side, by in ((even, 1 - parity, SCALE), (odd, parity, factor)):
        for m in range(margin):
            for k in range(4):
                first = (m * 4 + k) * 128
                store_pair(
                    ref[first : first + 128, :], high, low, side * (margin // 2) + m // 2, m % 2, k, by
                )
        base = margin * 512 + 8 * depth
        for m in range(margin):
            scaled[side * margin + m] = ref[base + 4 + m : base + 5 + m, :] * SCALE
            for k in range(1, 4):
                line = ref[base + k : base + k + 1, :]
                at_left, at_right = rows - margin + m, m
                one = jnp.where(
                    side == 0, line[:, at_left : at_left + 1], line[:, at_right : at_right + 1]
                )
                places[k - 1, side * margin + m] = jnp.broadcast_to(one, (1, 128))


class Chain:
    def __init__(self, rows, margin, steps, shifts, places, high, low, scaled, halo_parts=None):
        self.rows, self.margin, self.steps, self.shifts = rows, margin, steps, shifts
        self.places, self.high, self.low, self.scaled = places, high, low, scaled
        self.halo_parts = halo_parts
        self.mask = halves()

    def halo_at(self, row):
        return row + self.margin if row < 0 else self.margin + row - self.rows

    def mats(self, row):
        if 0 <= row < self.rows:
            return self.high[row // 2], self.low[row // 2]
        at = self.halo_at(row) // 2
        return self.halo_parts[0][at], self.halo_parts[1][at]

    def diagonal(self, row):
        if 0 <= row < self.rows:
            return self.scaled[row]
        return self.halo_parts[2][self.halo_at(row)]

    def gather(self, source, reach, row, k):
        if k == 0:
            return source[row + reach]
        if 0 <= row < self.rows:
            place = self.places[k - 1, row]
        else:
            place = self.halo_parts[3][k - 1, self.halo_at(row)]
        place = jnp.broadcast_to(place, (8, 128))
        total = source[row + W + reach]
        for c in (-W, 1 - W, W - 1):
            total = jnp.where(place == c, source[row + c + reach], total)
        return total

    def run(self, plan, values, known, splits, store):
        for step in range(self.steps):
            source, reach = splits[step], W * (self.steps - step)
            needed = {row + c for first in plan[step] for row in (first, first + 1) for c in range(-W, W + 1)}
            for row in sorted(needed & set(known[step])):
                source[row + reach] = split(values(step, row), self.mask)
            streamed = []
            for row in plan[step]:
                parts = []
                for k in range(4):
                    tiles = [self.gather(source, reach, row + h, k) for h in range(2)]
                    parts.append(jnp.concatenate(tiles, 0).astype(BF16))
                streamed.append(jnp.concatenate(parts, 1))
            sums = []
            for row, left in zip(plan[step], streamed):
                high, low = self.mats(row)
                sums.append(
                    jnp.dot(left, high, preferred_element_type=F32)
                    + jnp.dot(left, low, preferred_element_type=F32)
                )
            for row, total in zip(plan[step], sums):
                for h in range(2):
                    at = row + h
                    part = total[8 * h : 8 * h + 8, 128 * h : 128 * h + 128]
                    part = part + pltpu.roll(part, 4, 0)
                    tile = part + (self.diagonal(at) - SCALE * self.shifts[step]) * values(step, at)
                    store(step, at, tile)
                    if step < self.steps - 1:
                        splits[step + 1][at + reach - W] = split(tile, self.mask)


def inner_rows(rows, step):
    return list(range(W * step, rows - W * step)) if rows > 2 * W * step else []


def without(rows, done):
    return [row for row in rows[::2] if row not in set(done)]


def whole_rows(rows, steps, step):
    return list(range(-W * (steps - step), rows + W * (steps - step)))


def copy_rows(begun, outs, done):
    for old, new, rows in zip(begun, outs, done):
        for row in rows:
            new[row] = old[row]


def vector_access(rows, steps, own, outs, halo=None, inner=None):
    depth = W * steps

    def values(step, row):
        if 0 <= row < rows:
            return own[row] if step == 0 else outs[step - 1][row]
        if step == 0:
            return halo[0, row + depth] if row < 0 else halo[1, row - rows]
        keep = W * (steps - step)
        return inner[step - 1][row + keep if row < 0 else keep + row - rows]

    def store(step, row, tile):
        if 0 <= row < rows:
            outs[step][row] = tile
        else:
            keep = W * (steps - 1 - step)
            inner[step][row + keep if row < 0 else keep + row - rows] = tile

    return values, store


def convert_kernel(steps, shifts, *refs):
    blocks, rhs, diag, offs, start, scaled, places, high, low = refs[:9]
    outs, splits = refs[9 : 9 + steps], refs[9 + steps : 9 + 2 * steps]
    buf, sems = refs[9 + 2 * steps :]
    rows = buf.shape[0]

    def fetch(i):
        first = pl.multiple_of(i * 512, 512)
        return pltpu.make_async_copy(blocks.at[pl.ds(first, 512)], buf.at[i], sems.at[i])

    for i in range(rows):
        fetch(i).start()
    for i in range(rows):
        part = rhs[:, i * 128 : (i + 1) * 128]
        start[i] = jnp.concatenate([part, part], 0)
        scaled[i] = diag[i : i + 1, :] * SCALE
    turned = jnp.concatenate([offs[...].astype(F32), jnp.zeros((4, 128 - rows), F32)], 1)
    turned = jnp.concatenate([turned, jnp.zeros((4, 128), F32)], 0).T
    for k in range(1, 4):
        places[k - 1] = jnp.broadcast_to(turned[:rows, k : k + 1], (rows, 128)).reshape(rows, 1, 128)

    def body(p, carry):
        for half in range(2):
            i = 2 * p + half
            fetch(i).wait()
            for k in range(4):
                store_pair(buf[i, k * 128 : (k + 1) * 128, :], high, low, p, half, k)
        return carry

    lax.fori_loop(0, rows // 2, body, 0)
    chain = Chain(rows, 0, steps, shifts, places, high, low, scaled)
    plan = [without(inner_rows(rows, j + 1), []) for j in range(steps)]
    values, store = vector_access(rows, steps, start, outs)
    chain.run(plan, values, [range(rows)] + [[]] * (steps - 1), splits, store)


def inner_kernel(steps, shifts, done, earlier, *refs):
    places, high, low, scaled, own = refs[:5]
    refs = list(refs[5:])
    begun = refs[: len(done)]
    del refs[: len(done)]
    before = refs[:earlier]
    del refs[:earlier]
    outs = refs[:steps]
    del refs[:steps]
    rows = own.shape[0]
    if earlier:
        products = refs.pop(0)
        vectors = before + [own]
        tile = jnp.zeros((8, 128), F32)
        products[...] = add_products(tile, vectors, pair_blocks((earlier + 1) // 2, earlier + 1))
    splits = refs
    copy_rows(begun, outs, done)
    done = list(done) + [[]] * (steps - len(done))
    chain = Chain(rows, 0, steps, shifts, places, high, low, scaled)
    plan = [without(inner_rows(rows, j + 1), done[j]) for j in range(steps)]
    values, store = vector_access(rows, steps, own, outs)
    chain.run(plan, values, [range(rows)] + done[:-1], splits, store)


def rest_kernel(first, steps, shifts, margin, done, next_depth, earlier, *refs):
    refs = list(refs)
    places, high, low, scaled, own, from_even, from_odd = refs[:7]
    del refs[:7]
    begun = refs[:steps]
    del refs[:steps]
    if earlier:
        products, before = refs[0], refs[1 : 1 + earlier]
        del refs[: 1 + earlier]
    parts = refs[:4]
    del refs[:4]
    outs = refs[:steps]
    del refs[:steps]
    if earlier:
        gram = refs.pop(0)
    if next_depth:
        to_even, to_odd = refs[:2]
        del refs[:2]
    splits, halo, inner = refs[:steps], refs[steps], refs[steps + 1 :]
    rows = own.shape[0]
    depth = W * steps
    parity = lax.axis_index("dom") % 2
    if first:
        take_message(depth, margin, rows, parity, from_even, from_odd, *parts, halo)
    else:
        take_vectors(depth, parity, lambda i: from_even[i], lambda i: from_odd[i], halo)
    copy_rows(begun, outs, done)
    chain = Chain(rows, margin, steps, shifts, places, high, low, scaled, parts)
    plan = [without(whole_rows(rows, steps, j + 1), done[j]) for j in range(steps)]
    values, store = vector_access(rows, steps, own, outs, halo, inner)
    known = [range(-depth, rows + depth)] + list(done[:-1])
    chain.run(plan, values, known, splits, store)
    if next_depth:
        last = outs[-1]
        for i in range(next_depth):
            to_even[i] = last[(1 - parity) * (rows - next_depth) + i]
            to_odd[i] = last[parity * (rows - next_depth) + i]
    if earlier:
        vectors = list(before) + [own] + list(outs)
        new = [(i, j) for j in range(earlier + 1, earlier + 1 + steps) for i in range(j + 1)]
        tile = add_products(products[...], vectors, [new])
        gram[...] = tile + pltpu.roll(tile, 4, 0)


def pair_blocks(split, count):
    low, top = range(split), range(split, count)
    return (
        [(i, j) for i in low for j in low if i <= j],
        [(i, j) for i in low for j in top],
        [(i, j) for i in top for j in top if i <= j],
    )


PLACES = {pair: at for at, pair in enumerate((i, j) for j in range(CHAIN + 1) for i in range(j + 1))}


def dense(ref, p, mask):
    return jnp.where(mask, ref[2 * p], ref[2 * p + 1])


def add_products(tile, vectors, blocks):
    count = vectors[0].shape[0] // 2
    mask = halves()
    lane = lax.broadcasted_iota(jnp.int32, (8, 128), 1)
    for pairs in blocks:
        used = sorted({i for pair in pairs for i in pair})
        total = None
        for p in range(count):
            here = {i: dense(vectors[i], p, mask) for i in used}
            products = [here[i] * here[j] for i, j in pairs]
            total = products if total is None else [a + b for a, b in zip(total, products)]
        for pair, one in zip(pairs, total):
            tile = jnp.where(lane == PLACES[pair], jnp.sum(one, axis=1, keepdims=True), tile)
    return tile


def small_solve(gram):
    def g(i, j):
        return gram[(i, j) if i <= j else (j, i)]

    right = [[SHIFTS[b] * g(a, b) + GROW * g(a, b + 1) for b in range(S)] for a in range(S + 1)]
    normal = [
        [SHIFTS[a] * right[a][b] + GROW * right[a + 1][b] for b in range(a + 1)] for a in range(S)
    ]
    target = [SHIFTS[a] * g(a, 0) + GROW * g(a + 1, 0) for a in range(S)]
    lower = [[None] * S for _ in range(S)]
    scaled = [[None] * S for _ in range(S)]
    inverse = []
    for j in range(S):
        pivot = normal[j][j]
        for k in range(j):
            pivot = pivot - scaled[j][k] * lower[j][k]
        inverse.append(1.0 / pivot)
        for i in range(j + 1, S):
            entry = normal[i][j]
            for k in range(j):
                entry = entry - scaled[i][k] * lower[j][k]
            scaled[i][j] = entry
            lower[i][j] = entry * inverse[j]
    coeffs = list(target)
    for i in range(S):
        for k in range(i):
            coeffs[i] = coeffs[i] - lower[i][k] * coeffs[k]
    coeffs = [c * d for c, d in zip(coeffs, inverse)]
    for i in reversed(range(S)):
        for k in range(i + 1, S):
            coeffs[i] = coeffs[i] - lower[k][i] * coeffs[k]
    combine = []
    for m in range(S + 1):
        entry = jnp.ones_like(coeffs[0]) if m == 0 else -GROW * coeffs[m - 1]
        if m < S:
            entry = entry - SHIFTS[m] * coeffs[m]
        combine.append(entry)
    return coeffs, combine


def final_kernel(total_gram, *refs):
    vectors, solution_ref, residual_ref = refs[:-2], refs[-2], refs[-1]
    count = vectors[0].shape[0] // 2
    mask = halves()
    tile = total_gram[...]
    gram = {
        pair: jnp.broadcast_to(tile[:, at : at + 1], (8, 128)) for pair, at in PLACES.items()
    }

    def g(i, j):
        return gram[(i, j) if i <= j else (j, i)]

    coeffs, combine = small_solve(gram)
    columns = [combine]
    for k in range(S):
        last = columns[-1]
        column = []
        for m in range(len(last) + 1):
            entry = None
            if m < len(last):
                gap = SCALE * (SHIFTS[m % S] - SHIFTS[k])
                entry = gap * last[m] if m % S != k else None
            if m > 0:
                entry = last[m - 1] if entry is None else entry + last[m - 1]
            column.append(jnp.zeros_like(last[0]) if entry is None else entry)
        columns.append(column)
    second = {}
    for b in range(S + 1):
        image = []
        for m in range(len(columns[b])):
            total = None
            for i, c in enumerate(columns[b]):
                term = g(m, i) * c
                total = term if total is None else total + term
            image.append(total)
        for a in range(b + 1):
            total = None
            for m, c in enumerate(columns[a]):
                term = c * image[m]
                total = term if total is None else total + term
            second[(a, b)] = total
    more, ending = small_solve(second)
    to_solution, to_residual = [], []
    for m in range(CHAIN + 1):
        total = coeffs[m] if m < S else None
        for a in range(S):
            if m < len(columns[a]):
                term = more[a] * columns[a][m]
                total = term if total is None else total + term
        to_solution.append(total)
        total = None
        for a in range(S + 1):
            if m < len(columns[a]):
                term = ending[a] * columns[a][m]
                total = term if total is None else total + term
        to_residual.append(total)
    for p in range(count):
        here = [dense(ref, p, mask) for ref in vectors]
        for ref, weights in ((solution_ref, to_solution), (residual_ref, to_residual)):
            total = None
            for weight, one in zip(weights, here):
                if weight is not None:
                    total = weight * one if total is None else total + weight * one
            ref[:, (2 * p) * 128 : (2 * p + 1) * 128] = total[0:4]
            ref[:, (2 * p + 1) * 128 : (2 * p + 2) * 128] = total[4:8]


def shape(*dims, kind=F32):
    return jax.ShapeDtypeStruct(dims, kind)


def cost(block_rows):
    return pl.CostEstimate(flops=block_rows * 2**21, bytes_accessed=block_rows * 2**18, transcendentals=0)


def local(blocks, offsets, diag_shift, right_side):
    rhs_count = right_side.shape[0]
    rows, per_row, size = blocks.shape[0], blocks.shape[1], blocks.shape[2]
    count = lax.axis_size("dom")
    margin = W * (max(GROUPS) - 1)
    steps = GROUPS[0]
    depth = W * steps
    flat = pltpu.with_memory_space_constraint(blocks.reshape(rows * per_row * size, size), pltpu.HBM)
    offs = offsets.T
    diag = diag_shift.reshape(rows, size)
    message = shape(margin * 512 + 8 * depth + 8, size)
    even, odd = pl.pallas_call(
        functools.partial(prep_kernel, depth, margin),
        out_shape=[message, message],
        in_specs=[HB, HB, HB, HB],
        out_specs=[VM] * 2,
        scratch_shapes=[
            pltpu.VMEM(right_side.shape, F32),
            pltpu.VMEM(diag.shape, F32),
            pltpu.VMEM(offs.shape, jnp.int32),
            pltpu.SemaphoreType.DMA((5,)),
        ],
        compiler_params=params(8),
        name="prepare",
    )(
        flat,
        *[pltpu.with_memory_space_constraint(x, pltpu.HBM) for x in (right_side, diag, offs)],
    )

    swap_even = [(i, i ^ 1) for i in range(count)]
    copies = lax.axis_size("groups")
    swap_odd = [(g * count + i, g * count + i + 1) for g in range(copies) for i in range(1, count - 1, 2)]
    for end in (0, count - 1):
        swap_odd += [(g * count + end, (g + 1) * count + end) for g in range(0, copies - 1, 2)]
    swap_odd += [(b, a) for a, b in swap_odd]

    def exchange(even, odd):
        odd = lax.ppermute(odd, ("groups", "dom"), swap_odd)
        return lax.ppermute(even, "dom", swap_even), odd

    even, odd = exchange(even, odd)

    vector = shape(rows, 8, size)
    pair_shape = pltpu.VMEM((rows // 2, per_row * size, 2 * size), BF16)

    def buffers(steps):
        return [pltpu.VMEM((rows + 2 * W * (steps - j), 8, size), F32) for j in range(steps)]

    started = [inner_rows(rows, j + 1) for j in range(AHEAD)]
    start, scaled, places, high, low, *ahead = pl.pallas_call(
        functools.partial(convert_kernel, AHEAD, [SHIFTS[j % S] for j in range(AHEAD)]),
        out_shape=[vector, shape(rows, 1, size), shape(per_row - 1, rows, 1, size)]
        + [pair_shape] * 2
        + [vector] * AHEAD,
        in_specs=[HB, VM, VM, VM],
        out_specs=[VM] * (5 + AHEAD),
        scratch_shapes=buffers(AHEAD)
        + [pltpu.VMEM((rows, per_row * size, size), F32), pltpu.SemaphoreType.DMA((rows,))],
        compiler_params=params(24),
        cost_estimate=cost(2 * rows + sum(len(r) for r in started)),
        name="convert",
    )(flat, right_side, diag, offs)

    vectors = [start]
    halo_shape = pltpu.VMEM((margin, per_row * size, 2 * size), BF16)
    parts = None
    at = 0
    for number, steps in enumerate(GROUPS):
        shifts = [SHIFTS[(at + j) % S] for j in range(steps)]
        depth = W * steps
        begun, done = ahead[at : at + steps], started[at : at + steps]
        inner = [inner_rows(rows, j + 1) for j in range(steps)]
        last = number + 1 == len(GROUPS)
        before = vectors[:-1] if last else []
        if done != inner and (number > 1 or INNER_SECOND or not begun):
            begun = pl.pallas_call(
                functools.partial(inner_kernel, steps, shifts, done, len(before)),
                out_shape=[vector] * steps + [shape(8, size)] * last,
                in_specs=[VM] * (5 + len(begun) + len(before)),
                out_specs=[VM] * (steps + last),
                scratch_shapes=buffers(steps),
                compiler_params=params(16),
                cost_estimate=cost(sum(len(r) for r in inner)),
                name="inner",
            )(places, high, low, scaled, vectors[-1], *begun, *before)
            done = inner
            begun, products = begun[:steps], begun[steps:]
        next_depth = W * GROUPS[number + 1] if number + 1 < len(GROUPS) else 0
        first = number == 0
        outs = [vector] * steps + [shape(8, size)] * last + [shape(next_depth, 8, size)] * (0 if last else 2)
        if first:
            outs = [halo_shape, halo_shape, shape(2 * margin, 1, size), shape(per_row - 1, 2 * margin, 1, size)] + outs
        results = pl.pallas_call(
            functools.partial(rest_kernel, first, steps, shifts, margin, done, next_depth, len(before)),
            out_shape=outs,
            in_specs=[VM] * (7 + steps + (0 if first else 4) + (1 + len(before) if last else 0)),
            out_specs=[VM] * len(outs),
            scratch_shapes=buffers(steps)
            + [pltpu.VMEM((2, depth, 8, size), F32)]
            + [pltpu.VMEM((2 * W * (steps - 1 - j), 8, size), F32) for j in range(steps - 1)],
            compiler_params=params(16),
            cost_estimate=cost(16),
            name="rest",
        )(places, high, low, scaled, vectors[-1], even, odd, *begun, *((*products, *before) if last else ()), *(parts or []))
        results = list(results)
        if first:
            parts, results = results[:4], results[4:]
        vectors += results[:steps]
        at += steps
        if next_depth:
            even, odd = exchange(*results[steps:])

    gram = results[steps]
    if count & (count - 1):
        gram = lax.psum(gram, "dom")
    else:
        for stage in range(count.bit_length() - 1):
            gram = gram + lax.ppermute(gram, "dom", [(i, i ^ (1 << stage)) for i in range(count)])
    return tuple(
        pl.pallas_call(
            final_kernel,
            out_shape=[shape(rhs_count, rows * size)] * 2,
            in_specs=[VM] * (1 + len(vectors)),
            out_specs=[VM] * 2,
            compiler_params=params(16),
            name="finish",
        )(gram, *vectors)
    )


def solution(mesh):
    in_specs = (
        P(("groups", "dom"), None, None, None),
        P(("groups", "dom"), None),
        P(("groups", "dom")),
        P(None, ("groups", "dom")),
    )
    out_specs = (P(None, ("groups", "dom")), P(None, ("groups", "dom")))
    return jax.shard_map(local, mesh=mesh, in_specs=in_specs, out_specs=out_specs, check_vma=False)
```

```python
import functools
import math

import jax
import jax.numpy as jnp
import numpy as np
from jax import lax
from jax.experimental import pallas as pl
from jax.experimental.pallas import tpu as pltpu
from jax.sharding import PartitionSpec as P

W = 2
S = 6
CYCLES = 2
CHAIN = S * CYCLES
GROUPS = (3, 3, 3, 3)
SCALE = 0.125
GROW = 1.0 / SCALE
SHIFTS = [
    float(np.float32(1.6) + np.float32(0.8) * np.float32(math.cos(math.pi * (2 * j + 1) / (2 * S))))
    for j in range(S)
]
F32 = jnp.float32
BF16 = jnp.bfloat16
VM = pl.BlockSpec(memory_space=pltpu.VMEM)
HB = pl.BlockSpec(memory_space=pltpu.HBM)


def params(mib):
    return pltpu.CompilerParams(vmem_limit_bytes=mib << 20)


def halves():
    return lax.broadcasted_iota(jnp.int32, (8, 128), 0) < 4


def split(tile, mask):
    high = tile.astype(BF16).astype(F32)
    return jnp.where(mask, high, tile - high)


def store_pair(block, high_ref, low_ref, pair, half, k, factor=SCALE):
    block = block * factor
    high = block.astype(BF16)
    low = (block - high.astype(F32)).astype(BF16)
    rows, cols = slice(k * 128, (k + 1) * 128), slice(half * 128, (half + 1) * 128)
    high_ref[pair, rows, cols] = high.T
    low_ref[pair, rows, cols] = low.T


def neighbour_slots():
    return [(r, c) for r in range(2) for c in range(4) if (r, c) not in ((1, 0), (0, 3))] + [None]


def prep_kernel(blocks, diag, offs, even, odd, buf, diag_buf, offs_buf, sems):
    rows = diag.shape[0]
    parity = lax.axis_index("dom") % 2
    sides = ((even, 1 - parity), (odd, parity))
    small = [
        pltpu.make_async_copy(diag, diag_buf, sems.at[0]),
        pltpu.make_async_copy(offs, offs_buf, sems.at[1]),
    ]
    large = []
    for place, (ref, at) in enumerate(sides):
        first = pl.multiple_of(at * (rows - 2) * 512, 512)
        large.append(pltpu.make_async_copy(blocks.at[pl.ds(first, 1024)], buf.at[place], sems.at[2 + place]))
    for copy in large + small:
        copy.start()
    for copy in small:
        copy.wait()
    offsets = offs_buf[...].astype(F32)
    masks = []
    for ref, at in sides:
        last = at == 1
        places = jnp.where(last, offsets[:, rows - 2 :], offsets[:, :2])
        places = [
            [jnp.broadcast_to(places[k : k + 1, r : r + 1], (128, 128)) for k in range(4)] for r in range(2)
        ]
        own = jnp.where(last, diag_buf[rows - 2 :, :], diag_buf[:2, :])
        base = 128 * len(neighbour_slots())
        ref[base : base + 2, :] = own
        ref[base + 2 : base + 8, :] = jnp.zeros((6, 128), F32)
        masks.append((jnp.where(last, 0.0, -2.0), last, places))
    for number, (ref, at) in enumerate(sides):
        large[number].wait()
        shift, last, places = masks[number]
        parts = [[buf[number, (r * 4 + k) * 128 : (r * 4 + k + 1) * 128, :] for k in range(4)] for r in range(2)]

        def block(r, c):
            total = jnp.zeros((128, 128), F32)
            for k in range(4):
                total = jnp.where(places[r][k] == c - r + shift, parts[r][k], total)
            return total

        for at_slot, slot in enumerate(neighbour_slots()):
            here = jnp.where(last, block(1, 0), block(0, 3)) if slot is None else block(*slot)
            ref[at_slot * 128 : (at_slot + 1) * 128, :] = here


def at_inside():
    me = lax.axis_index("dom")
    return jnp.logical_and(me > 0, me < lax.axis_size("dom") - 1)


def take_vectors(parity, even, odd, halo):
    inside = at_inside()
    for i in range(even.shape[0]):
        halo[1 - parity, i] = even[i]
        tile = odd[i]
        halo[parity, i] = jnp.where(inside, tile, jnp.zeros_like(tile))


def take_message(parity, even, odd, high, low, scaled):
    factor = jnp.where(at_inside(), SCALE, 0.0)
    for ref, side, by in ((even, 1 - parity, SCALE), (odd, parity, factor)):
        left = side == 0
        for at_slot, slot in enumerate(neighbour_slots()):
            block = ref[at_slot * 128 : (at_slot + 1) * 128, :]
            if slot is None:
                none = jnp.zeros_like(block)
                store_pair(jnp.where(left, block, none), high, low, side, 1, 0, by)
                store_pair(jnp.where(left, none, block), high, low, side, 0, 3, by)
            else:
                store_pair(block, high, low, side, slot[0], slot[1], by)
        base = 128 * len(neighbour_slots())
        for r in range(2):
            scaled[side, r] = ref[base + r : base + r + 1, :] * SCALE


class Chain:
    def __init__(self, rows, shifts, places, high, low, scaled):
        self.rows, self.shifts = rows, shifts
        self.places, self.high, self.low, self.scaled = places, high, low, scaled
        self.mask = halves()

    def gather(self, source, row, k):
        if k == 0:
            return source[row + W]
        place = jnp.broadcast_to(self.places[k - 1, row], (8, 128))
        total = source[row + 2 * W]
        for c in (-W, 1 - W, W - 1):
            total = jnp.where(place == c, source[row + W + c], total)
        return total

    def fill(self, source, rows, value):
        for row in rows:
            source[row + W] = split(value(row), self.mask)

    def product(self, left, high, low):
        return jnp.dot(left, high, preferred_element_type=F32) + jnp.dot(left, low, preferred_element_type=F32)

    def part(self, total, h):
        part = total[8 * h : 8 * h + 8, 128 * h : 128 * h + 128]
        return part + pltpu.roll(part, 4, 0)

    def advance(self, step, pairs, source, value, emit, extra=()):
        streamed = []
        for row in pairs:
            parts = []
            for k in range(4):
                tiles = [self.gather(source, row + h, k) for h in range(2)]
                parts.append(jnp.concatenate(tiles, 0).astype(BF16))
            streamed.append(jnp.concatenate(parts, 1))
        more = [self.product(left, high, low) for left, high, low, _ in extra]
        sums = [self.product(left, self.high[row // 2], self.low[row // 2]) for row, left in zip(pairs, streamed)]
        for total, (_, _, _, use) in zip(more, extra):
            use(total)
        for row, total in zip(pairs, sums):
            for h in range(2):
                at = row + h
                emit(at, self.part(total, h) + (self.scaled[at] - SCALE * self.shifts[step]) * value(at))


def edge_pairs(rows, depth):
    return list(range(0, depth, 2)) + list(range(rows - depth, rows, 2))


def inner_rows(rows, step):
    return list(range(W * step, rows - W * step))


def around(pairs, rows):
    return sorted({p + c for p in pairs for c in range(-W, W + 2)} & set(range(rows)))


def send_edges(chain, steps, last, to_even, to_odd, sources):
    rows = chain.rows
    parity = lax.axis_index("dom") % 2
    values = {row: last[row] for row in around(edge_pairs(rows, W * steps), rows)}
    for step in range(steps):
        for h in range(2):
            low, top = values[h], values[rows - 2 + h]
            to_even[2 * step + h] = jnp.where(parity == 0, top, low)
            to_odd[2 * step + h] = jnp.where(parity == 0, low, top)
        if step == steps - 1:
            break
        source = sources[step]
        for row in (0, 1, rows + W, rows + W + 1):
            source[row] = jnp.zeros((8, 128), F32)
        pairs = edge_pairs(rows, W * (steps - 1 - step))
        chain.fill(source, around(pairs, rows), values.get)
        found = {}
        chain.advance(step, pairs, source, values.get, found.__setitem__)
        values = found


def convert_kernel(steps, shifts, *refs):
    blocks, rhs, diag, offs, start, scaled, places, high, low, to_even, to_odd = refs[:11]
    sources = refs[11 : 10 + steps]
    buf, sems = refs[10 + steps :]
    rows = buf.shape[0]

    def fetch(i):
        first = pl.multiple_of(i * 512, 512)
        return pltpu.make_async_copy(blocks.at[pl.ds(first, 512)], buf.at[i], sems.at[i])

    for i in range(rows):
        fetch(i).start()
    for i in range(rows):
        part = rhs[:, i * 128 : (i + 1) * 128]
        start[i] = jnp.concatenate([part, part], 0)
        scaled[i] = diag[i : i + 1, :] * SCALE
    turned = jnp.concatenate([offs[...].astype(F32), jnp.zeros((4, 128 - rows), F32)], 1)
    turned = jnp.concatenate([turned, jnp.zeros((4, 128), F32)], 0).T
    for k in range(1, 4):
        places[k - 1] = jnp.broadcast_to(turned[:rows, k : k + 1], (rows, 128)).reshape(rows, 1, 128)

    def body(p, carry):
        for half in range(2):
            i = 2 * p + half
            fetch(i).wait()
            for k in range(4):
                store_pair(buf[i, k * 128 : (k + 1) * 128, :], high, low, p, half, k)
        return carry

    lax.fori_loop(0, rows // 2, body, 0)
    chain = Chain(rows, shifts, places, high, low, scaled)
    send_edges(chain, steps, start, to_even, to_odd, sources)


def inner_kernel(steps, shifts, earlier, *refs):
    places, high, low, scaled, own = refs[:5]
    refs = list(refs[5:])
    before = refs[:earlier]
    del refs[:earlier]
    outs = refs[:steps]
    del refs[:steps]
    rows = own.shape[0]
    if earlier:
        products = refs.pop(0)
        vectors = before + [own]
        tile = jnp.zeros((8, 128), F32)
        products[...] = add_products(tile, vectors, pair_blocks((earlier + 1) // 2, earlier + 1))
    sources = refs
    chain = Chain(rows, shifts, places, high, low, scaled)
    chain.fill(sources[0], range(rows), lambda row: own[row])
    for step in range(steps):
        before = own if step == 0 else outs[step - 1]

        def emit(row, tile, step=step):
            outs[step][row] = tile
            if step < steps - 1:
                sources[step + 1][row + W] = split(tile, chain.mask)

        pairs = inner_rows(rows, step + 1)[::2]
        chain.advance(step, pairs, sources[step], lambda row, ref=before: ref[row], emit)


def rest_kernel(first, steps, shifts, next_steps, next_shifts, earlier, *refs):
    refs = list(refs)
    places, high, low, scaled, own, from_even, from_odd = refs[:7]
    del refs[:7]
    begun = refs[:steps]
    del refs[:steps]
    if first:
        bulk = refs[:2]
        del refs[:2]
    if earlier:
        products, before = refs[0], refs[1 : 1 + earlier]
        del refs[: 1 + earlier]
    side_high, side_low, side_scaled = refs[:3]
    del refs[:3]
    outs = refs[:steps]
    del refs[:steps]
    if earlier:
        gram = refs.pop(0)
    if next_steps:
        to_even, to_odd = refs[:2]
        del refs[:2]
    sources, halo = refs[:steps], refs[steps]
    more_sources = refs[steps + 1 :]
    rows = own.shape[0]
    parity = lax.axis_index("dom") % 2
    take_vectors(parity, from_even, from_odd, halo)
    if first:
        take_message(parity, *bulk, side_high, side_low, side_scaled)
    for j in range(steps):
        for row in inner_rows(rows, j + 1):
            outs[j][row] = begun[j][row]
    chain = Chain(rows, shifts, places, high, low, scaled)
    mask = chain.mask
    added = None
    for step in range(steps):
        source = sources[step]
        ref = own if step == 0 else outs[step - 1]
        pairs = edge_pairs(rows, W * (step + 1))
        known = around(pairs, rows)
        if step:
            known = [row for row in known if row in set(inner_rows(rows, step))]
        chain.fill(source, known, lambda row, ref=ref: ref[row])
        for side in range(2):
            for h in range(2):
                tile = halo[side, 2 * step + h]
                if added is not None:
                    tile = tile + added[side][h]
                source[h + side * (rows + W)] = split(tile, mask)
        extra, after = [], [[None] * 2 for _ in range(2)]
        if step < steps - 1:
            for side in range(2):
                near = [source[W + side * (rows - 2) + h] for h in range(2)]
                if added is None:
                    far = [jnp.zeros((8, 128), F32)] * 2
                else:
                    far = [split(tile, mask) for tile in added[side]]
                tiles = near + far if side else far + near
                left = jnp.concatenate([jnp.concatenate([t, t], 0).astype(BF16) for t in tiles], 1)

                def use(total, side=side, added=added, after=after, step=step):
                    for h in range(2):
                        tile = chain.part(total, h)
                        if added is not None:
                            tile = tile + (side_scaled[side, h] - SCALE * shifts[step]) * added[side][h]
                        after[side][h] = tile

                extra.append((left, side_high[side], side_low[side], use))

        def emit(row, tile, step=step):
            outs[step][row] = tile
            if step < steps - 1:
                sources[step + 1][row + W] = split(tile, mask)

        chain.advance(step, pairs, source, lambda row, ref=ref: ref[row], emit, extra)
        added = after
    if next_steps:
        chain = Chain(rows, next_shifts, places, high, low, scaled)
        send_edges(chain, next_steps, outs[-1], to_even, to_odd, more_sources)
    if earlier:
        vectors = list(before) + [own] + list(outs)
        new = [(i, j) for j in range(earlier + 1, earlier + 1 + steps) for i in range(j + 1)]
        tile = add_products(products[...], vectors, [new])
        gram[...] = tile + pltpu.roll(tile, 4, 0)


def pair_blocks(split, count):
    low, top = range(split), range(split, count)
    return (
        [(i, j) for i in low for j in low if i <= j],
        [(i, j) for i in low for j in top],
        [(i, j) for i in top for j in top if i <= j],
    )


PLACES = {pair: at for at, pair in enumerate((i, j) for j in range(CHAIN + 1) for i in range(j + 1))}


def dense(ref, p, mask):
    return jnp.where(mask, ref[2 * p], ref[2 * p + 1])


def add_products(tile, vectors, blocks):
    count = vectors[0].shape[0] // 2
    mask = halves()
    lane = lax.broadcasted_iota(jnp.int32, (8, 128), 1)
    for pairs in blocks:
        used = sorted({i for pair in pairs for i in pair})
        total = None
        for p in range(count):
            here = {i: dense(vectors[i], p, mask) for i in used}
            products = [here[i] * here[j] for i, j in pairs]
            total = products if total is None else [a + b for a, b in zip(total, products)]
        for pair, one in zip(pairs, total):
            tile = jnp.where(lane == PLACES[pair], jnp.sum(one, axis=1, keepdims=True), tile)
    return tile


def small_solve(gram):
    def g(i, j):
        return gram[(i, j) if i <= j else (j, i)]

    right = [[SHIFTS[b] * g(a, b) + GROW * g(a, b + 1) for b in range(S)] for a in range(S + 1)]
    normal = [
        [SHIFTS[a] * right[a][b] + GROW * right[a + 1][b] for b in range(a + 1)] for a in range(S)
    ]
    target = [SHIFTS[a] * g(a, 0) + GROW * g(a + 1, 0) for a in range(S)]
    lower = [[None] * S for _ in range(S)]
    scaled = [[None] * S for _ in range(S)]
    inverse = []
    for j in range(S):
        pivot = normal[j][j]
        for k in range(j):
            pivot = pivot - scaled[j][k] * lower[j][k]
        inverse.append(1.0 / pivot)
        for i in range(j + 1, S):
            entry = normal[i][j]
            for k in range(j):
                entry = entry - scaled[i][k] * lower[j][k]
            scaled[i][j] = entry
            lower[i][j] = entry * inverse[j]
    coeffs = list(target)
    for i in range(S):
        for k in range(i):
            coeffs[i] = coeffs[i] - lower[i][k] * coeffs[k]
    coeffs = [c * d for c, d in zip(coeffs, inverse)]
    for i in reversed(range(S)):
        for k in range(i + 1, S):
            coeffs[i] = coeffs[i] - lower[k][i] * coeffs[k]
    combine = []
    for m in range(S + 1):
        entry = jnp.ones_like(coeffs[0]) if m == 0 else -GROW * coeffs[m - 1]
        if m < S:
            entry = entry - SHIFTS[m] * coeffs[m]
        combine.append(entry)
    return coeffs, combine


def final_kernel(total_gram, *refs):
    vectors, solution_ref, residual_ref = refs[:-2], refs[-2], refs[-1]
    count = vectors[0].shape[0] // 2
    mask = halves()
    tile = total_gram[...]
    gram = {
        pair: jnp.broadcast_to(tile[:, at : at + 1], (8, 128)) for pair, at in PLACES.items()
    }

    def g(i, j):
        return gram[(i, j) if i <= j else (j, i)]

    coeffs, combine = small_solve(gram)
    columns = [combine]
    for k in range(S):
        last = columns[-1]
        column = []
        for m in range(len(last) + 1):
            entry = None
            if m < len(last):
                gap = SCALE * (SHIFTS[m % S] - SHIFTS[k])
                entry = gap * last[m] if m % S != k else None
            if m > 0:
                entry = last[m - 1] if entry is None else entry + last[m - 1]
            column.append(jnp.zeros_like(last[0]) if entry is None else entry)
        columns.append(column)
    second = {}
    for b in range(S + 1):
        image = []
        for m in range(len(columns[b])):
            total = None
            for i, c in enumerate(columns[b]):
                term = g(m, i) * c
                total = term if total is None else total + term
            image.append(total)
        for a in range(b + 1):
            total = None
            for m, c in enumerate(columns[a]):
                term = c * image[m]
                total = term if total is None else total + term
            second[(a, b)] = total
    more, ending = small_solve(second)
    to_solution, to_residual = [], []
    for m in range(CHAIN + 1):
        total = coeffs[m] if m < S else None
        for a in range(S):
            if m < len(columns[a]):
                term = more[a] * columns[a][m]
                total = term if total is None else total + term
        to_solution.append(total)
        total = None
        for a in range(S + 1):
            if m < len(columns[a]):
                term = ending[a] * columns[a][m]
                total = term if total is None else total + term
        to_residual.append(total)
    for p in range(count):
        here = [dense(ref, p, mask) for ref in vectors]
        for ref, weights in ((solution_ref, to_solution), (residual_ref, to_residual)):
            total = None
            for weight, one in zip(weights, here):
                if weight is not None:
                    total = weight * one if total is None else total + weight * one
            ref[:, (2 * p) * 128 : (2 * p + 1) * 128] = total[0:4]
            ref[:, (2 * p + 1) * 128 : (2 * p + 2) * 128] = total[4:8]


def shape(*dims, kind=F32):
    return jax.ShapeDtypeStruct(dims, kind)


def cost(block_rows):
    return pl.CostEstimate(flops=block_rows * 2**21, bytes_accessed=block_rows * 2**18, transcendentals=0)


def local(blocks, offsets, diag_shift, right_side):
    rhs_count = right_side.shape[0]
    rows, per_row, size = blocks.shape[0], blocks.shape[1], blocks.shape[2]
    count = lax.axis_size("dom")
    flat = pltpu.with_memory_space_constraint(blocks.reshape(rows * per_row * size, size), pltpu.HBM)
    offs = offsets.T
    diag = diag_shift.reshape(rows, size)
    message = shape(len(neighbour_slots()) * size + 8, size)
    even_blocks, odd_blocks = pl.pallas_call(
        prep_kernel,
        out_shape=[message, message],
        in_specs=[HB, HB, HB],
        out_specs=[VM] * 2,
        scratch_shapes=[
            pltpu.VMEM((2, 2 * per_row * size, size), F32),
            pltpu.VMEM(diag.shape, F32),
            pltpu.VMEM(offs.shape, jnp.int32),
            pltpu.SemaphoreType.DMA((4,)),
        ],
        compiler_params=params(16),
        name="prepare",
    )(flat, *[pltpu.with_memory_space_constraint(x, pltpu.HBM) for x in (diag, offs)])

    swap_even = [(i, i ^ 1) for i in range(count)]
    copies = lax.axis_size("groups")
    swap_odd = [(g * count + i, g * count + i + 1) for g in range(copies) for i in range(1, count - 1, 2)]
    for end in (0, count - 1):
        swap_odd += [(g * count + end, (g + 1) * count + end) for g in range(0, copies - 1, 2)]
    swap_odd += [(b, a) for a, b in swap_odd]

    def exchange(even, odd):
        odd = lax.ppermute(odd, ("groups", "dom"), swap_odd)
        return lax.ppermute(even, "dom", swap_even), odd

    bulk = exchange(even_blocks, odd_blocks)

    vector = shape(rows, 8, size)
    pair_shape = pltpu.VMEM((rows // 2, per_row * size, 2 * size), BF16)
    side_shape = pltpu.VMEM((2, per_row * size, 2 * size), BF16)
    source = pltpu.VMEM((rows + 2 * W, 8, size), F32)

    def shifts_from(at, steps):
        return [SHIFTS[(at + j) % S] for j in range(steps)]

    steps = GROUPS[0]
    edge = shape(2 * steps, 8, size)
    start, scaled, places, high, low, even, odd = pl.pallas_call(
        functools.partial(convert_kernel, steps, shifts_from(0, steps)),
        out_shape=[vector, shape(rows, 1, size), shape(per_row - 1, rows, 1, size)]
        + [pair_shape] * 2
        + [edge] * 2,
        in_specs=[HB, VM, VM, VM],
        out_specs=[VM] * 7,
        scratch_shapes=[source] * (steps - 1)
        + [pltpu.VMEM((rows, per_row * size, size), F32), pltpu.SemaphoreType.DMA((rows,))],
        compiler_params=params(24),
        cost_estimate=cost(2 * rows),
        name="convert",
    )(flat, right_side, diag, offs)

    vectors = [start]
    sides = None
    at = 0
    for number, steps in enumerate(GROUPS):
        even, odd = exchange(even, odd)
        shifts = shifts_from(at, steps)
        first, last = number == 0, number + 1 == len(GROUPS)
        before = vectors[:-1] if last else []
        begun = pl.pallas_call(
            functools.partial(inner_kernel, steps, shifts, len(before)),
            out_shape=[vector] * steps + [shape(8, size)] * last,
            in_specs=[VM] * (5 + len(before)),
            out_specs=[VM] * (steps + last),
            scratch_shapes=[source] * steps,
            compiler_params=params(16),
            cost_estimate=cost(sum(len(inner_rows(rows, j + 1)) for j in range(steps))),
            name="inner",
        )(places, high, low, scaled, vectors[-1], *before)
        begun, products = begun[:steps], begun[steps:]
        next_steps = 0 if last else GROUPS[number + 1]
        edge = shape(2 * next_steps, 8, size)
        outs = [vector] * steps + [shape(8, size)] * last + [edge] * (0 if last else 2)
        inputs = [places, high, low, scaled, vectors[-1], even, odd, *begun]
        if first:
            outs = [side_shape, side_shape, shape(2, 2, 1, size)] + outs
            inputs += bulk
        if last:
            inputs += [*products, *before]
        if not first:
            inputs += sides
        results = pl.pallas_call(
            functools.partial(
                rest_kernel,
                first,
                steps,
                shifts,
                next_steps,
                shifts_from(at + steps, next_steps),
                len(before),
            ),
            out_shape=outs,
            in_specs=[VM] * len(inputs),
            out_specs=[VM] * len(outs),
            scratch_shapes=[source] * steps
            + [pltpu.VMEM((2, 2 * steps, 8, size), F32)]
            + [source] * max(next_steps - 1, 0),
            compiler_params=params(16),
            cost_estimate=cost(16),
            name="rest",
        )(*inputs)
        results = list(results)
        if first:
            sides, results = results[:3], results[3:]
        vectors += results[:steps]
        at += steps
        if last:
            gram = results[steps]
        else:
            even, odd = results[steps:]

    if count & (count - 1):
        gram = lax.psum(gram, "dom")
    else:
        for stage in range(count.bit_length() - 1):
            gram = gram + lax.ppermute(gram, "dom", [(i, i ^ (1 << stage | 1)) for i in range(count)])
    return tuple(
        pl.pallas_call(
            final_kernel,
            out_shape=[shape(rhs_count, rows * size)] * 2,
            in_specs=[VM] * (1 + len(vectors)),
            out_specs=[VM] * 2,
            compiler_params=params(16),
            name="finish",
        )(gram, *vectors)
    )


def solution(mesh):
    in_specs = (
        P(("groups", "dom"), None, None, None),
        P(("groups", "dom"), None),
        P(("groups", "dom")),
        P(None, ("groups", "dom")),
    )
    out_specs = (P(None, ("groups", "dom")), P(None, ("groups", "dom")))
    return jax.shard_map(local, mesh=mesh, in_specs=in_specs, out_specs=out_specs, check_vma=False)
```

```python
import functools
import math

import jax
import jax.numpy as jnp
import numpy as np
from jax import lax
from jax.experimental import pallas as pl
from jax.experimental.pallas import tpu as pltpu
from jax.sharding import PartitionSpec as P

W = 2
S = 6
CYCLES = 2
CHAIN = S * CYCLES
GROUPS = (3, 3, 3, 3)
AHEAD = (3, 1, 0, 0)
PORTIONS = (3, 7, 11, 15, 18, 20)
SCALE = 0.125
GROW = 1.0 / SCALE
SHIFTS = [
    float(np.float32(1.6) + np.float32(0.8) * np.float32(math.cos(math.pi * (2 * j + 1) / (2 * S))))
    for j in range(S)
]
F32 = jnp.float32
BF16 = jnp.bfloat16
VM = pl.BlockSpec(memory_space=pltpu.VMEM)
HB = pl.BlockSpec(memory_space=pltpu.HBM)


def params(mib):
    return pltpu.CompilerParams(vmem_limit_bytes=mib << 20)


def halves():
    return lax.broadcasted_iota(jnp.int32, (8, 128), 0) < 4


def split(tile, mask):
    high = tile.astype(BF16).astype(F32)
    return jnp.where(mask, high, tile - high)


def store_pair(block, high_ref, low_ref, pair, half, k, factor=SCALE):
    block = block * factor
    high = block.astype(BF16)
    low = (block - high.astype(F32)).astype(BF16)
    rows, cols = slice(k * 128, (k + 1) * 128), slice(half * 128, (half + 1) * 128)
    high_ref[pair, rows, cols] = high.T
    low_ref[pair, rows, cols] = low.T


def neighbour_slots():
    return [(r, c) for r in range(2) for c in range(4) if (r, c) not in ((1, 0), (0, 3))] + [None]


def prep_kernel(blocks, diag, offs, even, odd, buf, diag_buf, offs_buf, sems):
    rows = diag.shape[0]
    parity = lax.axis_index("dom") % 2
    sides = ((even, 1 - parity), (odd, parity))
    small = [
        pltpu.make_async_copy(diag, diag_buf, sems.at[0]),
        pltpu.make_async_copy(offs, offs_buf, sems.at[1]),
    ]
    large = []
    for place, (ref, at) in enumerate(sides):
        first = pl.multiple_of(at * (rows - 2) * 512, 512)
        large.append(pltpu.make_async_copy(blocks.at[pl.ds(first, 1024)], buf.at[place], sems.at[2 + place]))
    for copy in large + small:
        copy.start()
    for copy in small:
        copy.wait()
    offsets = offs_buf[...].astype(F32)
    masks = []
    for ref, at in sides:
        last = at == 1
        places = jnp.where(last, offsets[:, rows - 2 :], offsets[:, :2])
        places = [
            [jnp.broadcast_to(places[k : k + 1, r : r + 1], (128, 128)) for k in range(4)] for r in range(2)
        ]
        own = jnp.where(last, diag_buf[rows - 2 :, :], diag_buf[:2, :])
        base = 128 * len(neighbour_slots())
        ref[base : base + 2, :] = own
        ref[base + 2 : base + 8, :] = jnp.zeros((6, 128), F32)
        masks.append((jnp.where(last, 0.0, -2.0), last, places))
    for number, (ref, at) in enumerate(sides):
        large[number].wait()
        shift, last, places = masks[number]
        parts = [[buf[number, (r * 4 + k) * 128 : (r * 4 + k + 1) * 128, :] for k in range(4)] for r in range(2)]

        def block(r, c):
            total = jnp.zeros((128, 128), F32)
            for k in range(4):
                total = jnp.where(places[r][k] == c - r + shift, parts[r][k], total)
            return total

        for at_slot, slot in enumerate(neighbour_slots()):
            here = jnp.where(last, block(1, 0), block(0, 3)) if slot is None else block(*slot)
            ref[at_slot * 128 : (at_slot + 1) * 128, :] = here


def at_inside():
    me = lax.axis_index("dom")
    return jnp.logical_and(me > 0, me < lax.axis_size("dom") - 1)


def take_vectors(parity, even, odd, halo):
    inside = at_inside()
    for i in range(even.shape[0]):
        halo[1 - parity, i] = even[i]
        tile = odd[i]
        halo[parity, i] = jnp.where(inside, tile, jnp.zeros_like(tile))


def take_message(parity, even, odd, high, low, scaled):
    factor = jnp.where(at_inside(), SCALE, 0.0)
    for ref, side, by in ((even, 1 - parity, SCALE), (odd, parity, factor)):
        left = side == 0
        for at_slot, slot in enumerate(neighbour_slots()):
            block = ref[at_slot * 128 : (at_slot + 1) * 128, :]
            if slot is None:
                none = jnp.zeros_like(block)
                store_pair(jnp.where(left, block, none), high, low, side, 1, 0, by)
                store_pair(jnp.where(left, none, block), high, low, side, 0, 3, by)
            else:
                store_pair(block, high, low, side, slot[0], slot[1], by)
        base = 128 * len(neighbour_slots())
        for r in range(2):
            scaled[side, r] = ref[base + r : base + r + 1, :] * SCALE


class Chain:
    def __init__(self, rows, shifts, places, high, low, scaled):
        self.rows, self.shifts = rows, shifts
        self.places, self.high, self.low, self.scaled = places, high, low, scaled
        self.mask = halves()

    def gather(self, source, row, k):
        if k == 0:
            return source[row + W]
        place = jnp.broadcast_to(self.places[k - 1, row], (8, 128))
        total = source[row + 2 * W]
        for c in (-W, 1 - W, W - 1):
            total = jnp.where(place == c, source[row + W + c], total)
        return total

    def fill(self, source, rows, value):
        for row in rows:
            source[row + W] = split(value(row), self.mask)

    def product(self, left, high, low):
        return jnp.dot(left, high, preferred_element_type=F32) + jnp.dot(left, low, preferred_element_type=F32)

    def part(self, total, h):
        part = total[8 * h : 8 * h + 8, 128 * h : 128 * h + 128]
        return part + pltpu.roll(part, 4, 0)

    def advance(self, step, pairs, source, value, emit, extra=()):
        streamed = []
        for row in pairs:
            parts = []
            for k in range(4):
                tiles = [self.gather(source, row + h, k) for h in range(2)]
                parts.append(jnp.concatenate(tiles, 0).astype(BF16))
            streamed.append(jnp.concatenate(parts, 1))
        more = [self.product(left, high, low) for left, high, low, _ in extra]
        sums = [self.product(left, self.high[row // 2], self.low[row // 2]) for row, left in zip(pairs, streamed)]
        for total, (_, _, _, use) in zip(more, extra):
            use(total)
        for row, total in zip(pairs, sums):
            for h in range(2):
                at = row + h
                emit(at, self.part(total, h) + (self.scaled[at] - SCALE * self.shifts[step]) * value(at))


def edge_pairs(rows, depth):
    return list(range(0, depth, 2)) + list(range(rows - depth, rows, 2))


def inner_rows(rows, step):
    return list(range(W * step, rows - W * step))


def around(pairs, rows):
    return sorted({p + c for p in pairs for c in range(-W, W + 2)} & set(range(rows)))


def send_edges(chain, steps, last, to_even, to_odd, sources):
    rows = chain.rows
    parity = lax.axis_index("dom") % 2
    values = {row: last[row] for row in around(edge_pairs(rows, W * steps), rows)}
    for step in range(steps):
        for h in range(2):
            low, top = values[h], values[rows - 2 + h]
            to_even[2 * step + h] = jnp.where(parity == 0, top, low)
            to_odd[2 * step + h] = jnp.where(parity == 0, low, top)
        if step == steps - 1:
            break
        source = sources[step]
        for row in (0, 1, rows + W, rows + W + 1):
            source[row] = jnp.zeros((8, 128), F32)
        pairs = edge_pairs(rows, W * (steps - 1 - step))
        chain.fill(source, around(pairs, rows), values.get)
        found = {}
        chain.advance(step, pairs, source, values.get, found.__setitem__)
        values = found


def convert_kernel(steps, shifts, *refs):
    blocks, rhs, diag, offs, start, scaled, places, high, low, to_even, to_odd = refs[:11]
    outs, sources = refs[11 : 11 + steps], refs[11 + steps : 11 + 2 * steps]
    buf, sems = refs[11 + 2 * steps :]
    rows = buf.shape[0]
    count = rows // 2

    def fetch(i):
        first = pl.multiple_of(i * 512, 512)
        return pltpu.make_async_copy(blocks.at[pl.ds(first, 512)], buf.at[i], sems.at[i])

    for i in range(rows):
        fetch(i).start()
    mask = halves()
    zero = jnp.zeros((8, 128), F32)
    for source in sources:
        for row in (0, 1, rows + W, rows + W + 1):
            source[row] = zero
    for i in range(rows):
        part = rhs[:, i * 128 : (i + 1) * 128]
        tile = jnp.concatenate([part, part], 0)
        start[i] = tile
        sources[0][i + W] = split(tile, mask)
        scaled[i] = diag[i : i + 1, :] * SCALE
    turned = jnp.concatenate([offs[...].astype(F32), jnp.zeros((4, 128 - rows), F32)], 1)
    turned = jnp.concatenate([turned, jnp.zeros((4, 128), F32)], 0).T
    for k in range(1, 4):
        places[k - 1] = jnp.broadcast_to(turned[:rows, k : k + 1], (rows, 128)).reshape(rows, 1, 128)
    chain = Chain(rows, shifts, places, high, low, scaled)
    values = [start] + list(outs)

    def take(step, pairs):
        def emit(row, tile):
            outs[step][row] = tile
            if step < steps - 1:
                sources[step + 1][row + W] = split(tile, mask)

        chain.advance(step, [2 * q for q in pairs], sources[step], lambda row: values[step][row], emit)

    portions = [count * part // PORTIONS[-1] for part in PORTIONS]
    taken = [0] * steps
    before = 0
    for until in portions + [count]:
        for p in range(before, until):
            for half in range(2):
                fetch(2 * p + half).wait()
        ready = before
        for step in range(steps):
            if step:
                ready = count if taken[step - 1] == count else max(taken[step - 1] - 1, 0)
            if step == steps - 1:
                ready = min(ready, count - steps)
            take(step, range(taken[step], max(ready, taken[step])))
            taken[step] = max(ready, taken[step])
        for p in range(before, until):
            for half in range(2):
                for k in range(4):
                    store_pair(buf[2 * p + half, k * 128 : (k + 1) * 128, :], high, low, p, half, k)
        before = until
    parity = lax.axis_index("dom") % 2
    for step in range(steps):
        for h in range(2):
            low_edge, top_edge = values[step][h], values[step][rows - 2 + h]
            to_even[2 * step + h] = jnp.where(parity == 0, top_edge, low_edge)
            to_odd[2 * step + h] = jnp.where(parity == 0, low_edge, top_edge)


def inner_kernel(steps, shifts, base, done, earlier, *refs):
    places, high, low, scaled, own = refs[:5]
    refs = list(refs[5:])
    begun = refs[: len(done)]
    del refs[: len(done)]
    before = refs[:earlier]
    del refs[:earlier]
    outs = refs[:steps]
    del refs[:steps]
    rows = scaled.shape[0]
    if earlier:
        products = refs.pop(0)
        vectors = before + [own]
        tile = jnp.zeros((8, 128), F32)
        products[...] = add_products(tile, vectors, pair_blocks((earlier + 1) // 2, earlier + 1))
    sources = refs
    chain = Chain(rows, shifts, places, high, low, scaled)
    done = list(done) + [[]] * (steps - len(done))
    for step, old in enumerate(begun):
        for row in done[step]:
            outs[step][row] = old[row]
    for step in range(steps):
        ref = own if step == 0 else outs[step - 1]
        pairs = [row for row in range(base + W * (step + 1), rows - base - W * (step + 1)) if row not in done[step]][::2]
        there = set(range(rows)) if step == 0 else set(done[step - 1])
        chain.fill(sources[step], [row for row in around(pairs, rows) if row in there], lambda row, ref=ref: ref[row])

        def emit(row, tile, step=step):
            outs[step][row] = tile
            if step < steps - 1:
                sources[step + 1][row + W] = split(tile, chain.mask)

        chain.advance(step, pairs, sources[step], lambda row, ref=ref: ref[row], emit)


def rest_kernel(first, steps, shifts, next_steps, next_shifts, earlier, unused, *refs):
    refs = list(refs)
    places, high, low, scaled, own, from_even, from_odd = refs[:7]
    del refs[:7]
    begun = refs[:steps]
    del refs[:steps]
    if first:
        bulk = refs[:2]
        del refs[:2]
    if earlier:
        products, before = refs[0], refs[1 : 1 + earlier]
        del refs[: 1 + earlier]
    if first:
        del refs[:unused]
    side_high, side_low, side_scaled = refs[:3]
    del refs[:3]
    if not first:
        del refs[:unused]
    outs = refs[:steps]
    del refs[:steps]
    if earlier:
        gram = refs.pop(0)
    if next_steps:
        to_even, to_odd = refs[:2]
        del refs[:2]
    sources, halo = refs[:steps], refs[steps]
    more_sources = refs[steps + 1 :]
    rows = own.shape[0]
    parity = lax.axis_index("dom") % 2
    take_vectors(parity, from_even, from_odd, halo)
    if first:
        take_message(parity, *bulk, side_high, side_low, side_scaled)
    for j in range(steps):
        for row in inner_rows(rows, j + 1):
            outs[j][row] = begun[j][row]
    chain = Chain(rows, shifts, places, high, low, scaled)
    mask = chain.mask
    added = None
    for step in range(steps):
        source = sources[step]
        ref = own if step == 0 else outs[step - 1]
        pairs = edge_pairs(rows, W * (step + 1))
        known = around(pairs, rows)
        if step:
            known = [row for row in known if row in set(inner_rows(rows, step))]
        chain.fill(source, known, lambda row, ref=ref: ref[row])
        for side in range(2):
            for h in range(2):
                tile = halo[side, 2 * step + h]
                if added is not None:
                    tile = tile + added[side][h]
                source[h + side * (rows + W)] = split(tile, mask)
        extra, after = [], [[None] * 2 for _ in range(2)]
        if step < steps - 1:
            for side in range(2):
                near = [source[W + side * (rows - 2) + h] for h in range(2)]
                far = [] if added is None else [split(tile, mask) for tile in added[side]]
                tiles = near + far if side else far + near
                columns = slice(None)
                if added is None:
                    columns = slice(0, 256) if side else slice(256, 512)
                left = jnp.concatenate([jnp.concatenate([t, t], 0).astype(BF16) for t in tiles], 1)

                def use(total, side=side, added=added, after=after, step=step):
                    for h in range(2):
                        tile = chain.part(total, h)
                        if added is not None:
                            tile = tile + (side_scaled[side, h] - SCALE * shifts[step]) * added[side][h]
                        after[side][h] = tile

                extra.append((left, side_high[side, columns], side_low[side, columns], use))

        def emit(row, tile, step=step):
            outs[step][row] = tile
            if step < steps - 1:
                sources[step + 1][row + W] = split(tile, mask)

        chain.advance(step, pairs, source, lambda row, ref=ref: ref[row], emit, extra)
        added = after
    if next_steps:
        chain = Chain(rows, next_shifts, places, high, low, scaled)
        send_edges(chain, next_steps, outs[-1], to_even, to_odd, more_sources)
    if earlier:
        vectors = list(before) + [own] + list(outs)
        new = [(i, j) for j in range(earlier + 1, earlier + 1 + steps) for i in range(j + 1)]
        tile = add_products(products[...], vectors, [new])
        gram[...] = tile + pltpu.roll(tile, 4, 0)


def pair_blocks(split, count):
    low, top = range(split), range(split, count)
    return (
        [(i, j) for i in low for j in low if i <= j],
        [(i, j) for i in low for j in top],
        [(i, j) for i in top for j in top if i <= j],
    )


PLACES = {pair: at for at, pair in enumerate((i, j) for j in range(CHAIN + 1) for i in range(j + 1))}


def dense(ref, p, mask):
    return jnp.where(mask, ref[2 * p], ref[2 * p + 1])


def add_products(tile, vectors, blocks):
    count = vectors[0].shape[0] // 2
    mask = halves()
    lane = lax.broadcasted_iota(jnp.int32, (8, 128), 1)
    for pairs in blocks:
        used = sorted({i for pair in pairs for i in pair})
        total = None
        for p in range(count):
            here = {i: dense(vectors[i], p, mask) for i in used}
            products = [here[i] * here[j] for i, j in pairs]
            total = products if total is None else [a + b for a, b in zip(total, products)]
        for pair, one in zip(pairs, total):
            tile = jnp.where(lane == PLACES[pair], jnp.sum(one, axis=1, keepdims=True), tile)
    return tile


def small_solve(gram):
    def g(i, j):
        return gram[(i, j) if i <= j else (j, i)]

    right = [[SHIFTS[b] * g(a, b) + GROW * g(a, b + 1) for b in range(S)] for a in range(S + 1)]
    normal = [
        [SHIFTS[a] * right[a][b] + GROW * right[a + 1][b] for b in range(a + 1)] for a in range(S)
    ]
    target = [SHIFTS[a] * g(a, 0) + GROW * g(a + 1, 0) for a in range(S)]
    lower = [[None] * S for _ in range(S)]
    scaled = [[None] * S for _ in range(S)]
    inverse = []
    for j in range(S):
        pivot = normal[j][j]
        for k in range(j):
            pivot = pivot - scaled[j][k] * lower[j][k]
        inverse.append(1.0 / pivot)
        for i in range(j + 1, S):
            entry = normal[i][j]
            for k in range(j):
                entry = entry - scaled[i][k] * lower[j][k]
            scaled[i][j] = entry
            lower[i][j] = entry * inverse[j]
    coeffs = list(target)
    for i in range(S):
        for k in range(i):
            coeffs[i] = coeffs[i] - lower[i][k] * coeffs[k]
    coeffs = [c * d for c, d in zip(coeffs, inverse)]
    for i in reversed(range(S)):
        for k in range(i + 1, S):
            coeffs[i] = coeffs[i] - lower[k][i] * coeffs[k]
    combine = []
    for m in range(S + 1):
        entry = jnp.ones_like(coeffs[0]) if m == 0 else -GROW * coeffs[m - 1]
        if m < S:
            entry = entry - SHIFTS[m] * coeffs[m]
        combine.append(entry)
    return coeffs, combine


def final_kernel(total_gram, *refs):
    vectors, solution_ref, residual_ref = refs[:-2], refs[-2], refs[-1]
    count = vectors[0].shape[0] // 2
    mask = halves()
    tile = total_gram[...]
    gram = {
        pair: jnp.broadcast_to(tile[:, at : at + 1], (8, 128)) for pair, at in PLACES.items()
    }

    def g(i, j):
        return gram[(i, j) if i <= j else (j, i)]

    coeffs, combine = small_solve(gram)
    columns = [combine]
    for k in range(S):
        last = columns[-1]
        column = []
        for m in range(len(last) + 1):
            entry = None
            if m < len(last):
                gap = SCALE * (SHIFTS[m % S] - SHIFTS[k])
                entry = gap * last[m] if m % S != k else None
            if m > 0:
                entry = last[m - 1] if entry is None else entry + last[m - 1]
            column.append(jnp.zeros_like(last[0]) if entry is None else entry)
        columns.append(column)
    second = {}
    for b in range(S + 1):
        image = []
        for m in range(len(columns[b])):
            total = None
            for i, c in enumerate(columns[b]):
                term = g(m, i) * c
                total = term if total is None else total + term
            image.append(total)
        for a in range(b + 1):
            total = None
            for m, c in enumerate(columns[a]):
                term = c * image[m]
                total = term if total is None else total + term
            second[(a, b)] = total
    more, ending = small_solve(second)
    to_solution, to_residual = [], []
    for m in range(CHAIN + 1):
        total = coeffs[m] if m < S else None
        for a in range(S):
            if m < len(columns[a]):
                term = more[a] * columns[a][m]
                total = term if total is None else total + term
        to_solution.append(total)
        total = None
        for a in range(S + 1):
            if m < len(columns[a]):
                term = ending[a] * columns[a][m]
                total = term if total is None else total + term
        to_residual.append(total)
    for p in range(count):
        here = [dense(ref, p, mask) for ref in vectors]
        for ref, weights in ((solution_ref, to_solution), (residual_ref, to_residual)):
            total = None
            for weight, one in zip(weights, here):
                if weight is not None:
                    total = weight * one if total is None else total + weight * one
            ref[:, (2 * p) * 128 : (2 * p + 1) * 128] = total[0:4]
            ref[:, (2 * p + 1) * 128 : (2 * p + 2) * 128] = total[4:8]


def shape(*dims, kind=F32):
    return jax.ShapeDtypeStruct(dims, kind)


def cost(block_rows):
    return pl.CostEstimate(flops=block_rows * 2**21, bytes_accessed=block_rows * 2**18, transcendentals=0)


def local(blocks, offsets, diag_shift, right_side):
    rhs_count = right_side.shape[0]
    rows, per_row, size = blocks.shape[0], blocks.shape[1], blocks.shape[2]
    count = lax.axis_size("dom")
    flat = pltpu.with_memory_space_constraint(blocks.reshape(rows * per_row * size, size), pltpu.HBM)
    offs = offsets.T
    diag = diag_shift.reshape(rows, size)
    message = shape(len(neighbour_slots()) * size + 8, size)
    even_blocks, odd_blocks = pl.pallas_call(
        prep_kernel,
        out_shape=[message, message],
        in_specs=[HB, HB, HB],
        out_specs=[VM] * 2,
        scratch_shapes=[
            pltpu.VMEM((2, 2 * per_row * size, size), F32),
            pltpu.VMEM(diag.shape, F32),
            pltpu.VMEM(offs.shape, jnp.int32),
            pltpu.SemaphoreType.DMA((4,)),
        ],
        compiler_params=params(16),
        name="prepare",
    )(flat, *[pltpu.with_memory_space_constraint(x, pltpu.HBM) for x in (diag, offs)])

    swap_even = [(i, i ^ 1) for i in range(count)]
    copies = lax.axis_size("groups")
    swap_odd = [(g * count + i, g * count + i + 1) for g in range(copies) for i in range(1, count - 1, 2)]
    for end in (0, count - 1):
        swap_odd += [(g * count + end, (g + 1) * count + end) for g in range(0, copies - 1, 2)]
    swap_odd += [(b, a) for a, b in swap_odd]

    def exchange(even, odd):
        odd = lax.ppermute(odd, ("groups", "dom"), swap_odd)
        return lax.ppermute(even, "dom", swap_even), odd

    bulk = exchange(even_blocks, odd_blocks)

    vector = shape(rows, 8, size)
    pair_shape = pltpu.VMEM((rows // 2, per_row * size, 2 * size), BF16)
    side_shape = pltpu.VMEM((2, per_row * size, 2 * size), BF16)
    source = pltpu.VMEM((rows + 2 * W, 8, size), F32)

    def shifts_from(at, steps):
        return [SHIFTS[(at + j) % S] for j in range(steps)]

    steps = GROUPS[0]
    edge = shape(2 * steps, 8, size)
    start, scaled, places, high, low, even, odd, *begun = pl.pallas_call(
        functools.partial(convert_kernel, steps, shifts_from(0, steps)),
        out_shape=[vector, shape(rows, 1, size), shape(per_row - 1, rows, 1, size)]
        + [pair_shape] * 2
        + [edge] * 2
        + [vector] * steps,
        in_specs=[HB, VM, VM, VM],
        out_specs=[VM] * (7 + steps),
        scratch_shapes=[source] * steps
        + [pltpu.VMEM((rows, per_row * size, size), F32), pltpu.SemaphoreType.DMA((rows,))],
        compiler_params=params(24),
        cost_estimate=cost(2 * rows),
        name="convert",
    )(flat, right_side, diag, offs)

    def inner(steps, shifts, base, done, earlier, own, *more):
        last = bool(earlier)
        return pl.pallas_call(
            functools.partial(inner_kernel, steps, shifts, base, done, earlier),
            out_shape=[vector] * steps + [shape(8, size)] * last,
            in_specs=[VM] * (5 + len(more)),
            out_specs=[VM] * (steps + last),
            scratch_shapes=[source] * steps,
            compiler_params=params(16),
            cost_estimate=cost(2 * rows),
            name="inner",
        )(places, high, low, scaled, own, *more)

    vectors = [start]
    sides = None
    at = 0
    done, ahead = [], []
    for number, steps in enumerate(GROUPS):
        even, odd = exchange(even, odd)
        shifts = shifts_from(at, steps)
        first, last = number == 0, number + 1 == len(GROUPS)
        before = vectors[:-1] if last else []
        products = []
        if not first:
            begun = inner(steps, shifts, 0, done, len(before), vectors[-1], *ahead, *before)
            begun, products = begun[:steps], begun[steps:]
        base, some = W * steps, AHEAD[number]
        ahead = []
        if some:
            ahead = list(inner(some, shifts_from(at + steps, some), base, [], 0, begun[-1]))
        done = [list(range(base + W * (j + 1), rows - base - W * (j + 1))) for j in range(some)]
        next_steps = 0 if last else GROUPS[number + 1]
        edge = shape(2 * next_steps, 8, size)
        outs = [vector] * steps + [shape(8, size)] * last + [edge] * (0 if last else 2)
        inputs = [places, high, low, scaled, vectors[-1], even, odd, *begun]
        if first:
            outs = [side_shape, side_shape, shape(2, 2, 1, size)] + outs
            inputs += bulk
        if last:
            inputs += [*products, *before]
        if not first:
            inputs += sides
        inputs += ahead[:1]
        results = pl.pallas_call(
            functools.partial(
                rest_kernel,
                first,
                steps,
                shifts,
                next_steps,
                shifts_from(at + steps, next_steps),
                len(before),
                len(ahead[:1]),
            ),
            out_shape=outs,
            in_specs=[VM] * len(inputs),
            out_specs=[VM] * len(outs),
            scratch_shapes=[source] * steps
            + [pltpu.VMEM((2, 2 * steps, 8, size), F32)]
            + [source] * max(next_steps - 1, 0),
            compiler_params=params(16),
            cost_estimate=cost(16),
            name="rest",
        )(*inputs)
        results = list(results)
        if first:
            sides, results = results[:3], results[3:]
        vectors += results[:steps]
        at += steps
        if last:
            gram = results[steps]
        else:
            even, odd = results[steps:]

    if count & (count - 1):
        gram = lax.psum(gram, "dom")
    else:
        for stage in range(count.bit_length() - 1):
            gram = gram + lax.ppermute(gram, "dom", [(i, i ^ (1 << stage | 1)) for i in range(count)])
    return tuple(
        pl.pallas_call(
            final_kernel,
            out_shape=[shape(rhs_count, rows * size)] * 2,
            in_specs=[VM] * (1 + len(vectors)),
            out_specs=[VM] * 2,
            compiler_params=params(16),
            name="finish",
        )(gram, *vectors)
    )


def solution(mesh):
    in_specs = (
        P(("groups", "dom"), None, None, None),
        P(("groups", "dom"), None),
        P(("groups", "dom")),
        P(None, ("groups", "dom")),
    )
    out_specs = (P(None, ("groups", "dom")), P(None, ("groups", "dom")))
    return jax.shard_map(local, mesh=mesh, in_specs=in_specs, out_specs=out_specs, check_vma=False)
```
